512 devices in a mesh: tile: 64 (over x, z, core), lev: 8 (over y).
Axes of the slice: x: 4, y: 8, z: 8, core: 2. Of those that a mesh axis runs over, the one named last changes fastest.
Arguments:
- grid_state: bfloat16 [8, 8192, 512], P('lev', 'tile'), may hold values from -28 to 28
- observations: bfloat16 [32768, 256], P('tile'), may hold values from -28 to 28
- destination: int32 [32768, 1], P('tile'), may hold values from 0 to 63; in each aligned block of 512 rows (0 to 511, 512 to 1023, ...) at most 16 rows name the same one
- subtile: int32 [32768], P('tile'), may hold values from 0 to 3
- query_weight: bfloat16 [512, 512], replicated, may hold values from -0.25 to 0.25
- key_weight: bfloat16 [256, 512], replicated, may hold values from -0.375 to 0.375
- value_weight: bfloat16 [256, 512], replicated, may hold values from -0.375 to 0.375
- out_weight: bfloat16 [512, 512], replicated, may hold values from -0.25 to 0.25
- sink_logit: float32 [8], replicated, may hold values from 0 to 4
- norm_gain: float32 [512], replicated, may hold values from 0.1 to 1.9
- mixing: float32 [8, 8], replicated, may hold values from -2 to 2
- up_weight: bfloat16 [512, 1024], replicated, may hold values from -0.25 to 0.25
- down_weight: bfloat16 [1024, 512], replicated, may hold values from -0.1875 to 0.1875
Outputs:
- analysis: bfloat16 [8, 8192, 512], P('lev', 'tile')
The draws below stay inside these ranges and needn't reach their ends.
Inputs may be any that keep to these rules, and one draw needn't show every extreme that they name: `destination`: at most 16 of the tokens of one tile shard name one tile, a bound that some block reaches of them.
All inputs are finite; a program needn't handle non-finite values.
Results may differ from the reference program's by a relative error of at most 0.006.
The reference program's roundings to bfloat16 on the way (of `queries`, `token_keys`, `token_values`, `probability`, `attended`, `updated`, `blended` and `hidden`) count: a program that leaves them out, or rounds other values in their place, can miss the bound.
Values may be sent and summed in bfloat16 or wider, within the bound.
No kernel may reach another device: no remote copies, remote signals or barrier semaphores. Data moves between devices by JAX's collectives and lax.ppermute only.
A program may use at most 64 MiB of HBM per device.

```python
import math
import jax
import jax.numpy as jnp
import numpy as np
from jax import lax

DG = 512
DO = 256
HEADS = 8
FF = 1024
SUBCELLS = 32
TOK_DEV = 512
CELL_DEV = 128
LEVELS = 8
CELLS = 8192
TOKENS = 32768
CAP = 16
RECV = 1024
SUBT = 4
N_TILE = 64


def draw_grid_state(key, part):
    key = jax.random.fold_in(key, 11)
    shape = (LEVELS, CELLS, DG)
    field = jnp.clip(jax.random.normal(key, shape, jnp.float32), -6.0, 6.0)
    return field.astype(jnp.bfloat16)


def draw_observations(key, part):
    key = jax.random.fold_in(key, 23)
    shape = (TOKENS, DO)
    field = jnp.clip(jax.random.normal(key, shape, jnp.float32), -6.0, 6.0)
    return field.astype(jnp.bfloat16)


def touch_ends(array, stream_key, smallest, high):
    longest = array.shape.index(max(array.shape))
    spots = []
    for shift in (0, 1):
        where = [jax.random.randint(jax.random.fold_in(stream_key, axis), (), 0, length) for axis, length in enumerate(array.shape)]
        where[longest] = (where[longest] + shift) % array.shape[longest]
        spots.append(tuple(where))
    return array.at[spots[0]].set(smallest).at[spots[1]].set(high)


def shared_out(stream_key, own, number, rows, amount, top, limit, lean):
    sequence = jax.random.permutation(stream_key, amount)
    heavy_load, usual = portions_of(amount, rows * top, limit, lean, True), portions_of(amount, rows * top, limit, lean, False)
    places = jnp.arange(amount)

    def named(lengths, offset_by):
        used = int((lengths > 0).sum())
        fixed = max(1, used // 4)
        passed = fixed + (places - fixed + offset_by * (used - fixed)) % max(1, amount - fixed)
        return jnp.zeros((amount,), jnp.int32).at[sequence[jnp.where(places < fixed, places, passed)]].set(jnp.asarray(lengths, jnp.int32))

    lengths = jnp.where(number % 4 == 0, named(heavy_load, number // 4), named(usual, number - number // 4 - 1))
    mixed = jax.random.permutation(jax.random.fold_in(own, 3), amount)
    source_of, sink = mixed[0:amount // 2 * 2:2], mixed[1:amount // 2 * 2:2]
    room = jnp.minimum(lengths[source_of] - 1, limit - lengths[sink]) // 2
    room = jnp.where((source_of == sequence[0]) | (sink == sequence[0]) | (lengths[sink] == 0), 0, jnp.maximum(room, 0))
    passed = jax.random.randint(jax.random.fold_in(own, 4), (amount // 2,), 0, 1 << 20) % (room + 1)
    lengths = lengths.at[source_of].add(-passed).at[sink].add(passed)
    items = jnp.searchsorted(jnp.cumsum(lengths), jnp.arange(rows * top), side="right").astype(jnp.int32)
    grid = items.reshape(top, rows).T
    grid = grid[jax.random.permutation(jax.random.fold_in(own, 1), rows)]
    offset_by = jax.random.randint(jax.random.fold_in(own, 2), (rows, 1), 0, top)
    return jnp.take_along_axis(grid, (jnp.arange(top)[None, :] + offset_by) % top, axis=1)


def portions_of(amount, total, reach, lean, full):
    loads = [(1 << 20) // math.isqrt(standing ** lean) + 1 for standing in range(1, amount + 1)]
    largest = reach if full else min(reach, max(-(-total // amount), total * loads[0] // sum(loads)))
    least = 1 if total - largest >= amount - 1 else 0
    counts, surplus = [largest] + [least] * (amount - 1), total - largest - least * (amount - 1)
    while surplus > 0:
        movable = [i for i in range(1, amount) if counts[i] < largest] or [i for i in range(1, amount) if counts[i] < reach]
        mass, remaining = sum([loads[i] for i in movable]), surplus
        for i in movable:
            addition = min(reach - counts[i], max(1, remaining * loads[i] // mass), surplus)
            counts[i] = counts[i] + addition
            surplus = surplus - addition
    return np.array(counts)


def normal_values(own_key, shape, deviation, bound, kind=jnp.bfloat16):
    return jnp.clip(deviation * jax.random.normal(own_key, shape, jnp.float32), -bound, bound).astype(kind)


def setup_inputs(seed: int = 0) -> dict:
    arg_keys = jax.random.split(jax.random.key(seed), 14)
    grid_state = draw_grid_state(jax.random.fold_in(arg_keys[13], 71), 0)
    observations = draw_observations(jax.random.fold_in(arg_keys[13], 71), 0)
    destination_keys = jax.random.split(jax.random.fold_in(arg_keys[2], 1), TOKENS // TOK_DEV)
    destination_turns = jax.random.permutation(jax.random.fold_in(arg_keys[2], 3), TOKENS // TOK_DEV)
    destination = jax.vmap(lambda own, number: shared_out(jax.random.fold_in(arg_keys[2], 2), own, number, TOK_DEV, N_TILE, 1, CAP, 2))(destination_keys, destination_turns).reshape((TOKENS, 1))
    subtile = touch_ends(jax.random.randint(arg_keys[3], (TOKENS,), 0, SUBT), jax.random.fold_in(arg_keys[3], 1), 0, SUBT - 1).astype(jnp.int32)
    query_weight = normal_values(arg_keys[4], (DG, DG), DG ** -0.5, 0.25)
    key_weight = normal_values(arg_keys[5], (DO, DG), DO ** -0.5, 0.375)
    value_weight = normal_values(arg_keys[6], (DO, DG), DO ** -0.5, 0.375)
    out_weight = normal_values(arg_keys[7], (DG, DG), DG ** -0.5, 0.25)
    sink_logit = jnp.clip(jax.random.uniform(arg_keys[8], (HEADS,), jnp.float32, 0.0, 4.0), 0.0, 4.0)
    norm_gain = jnp.clip(1.0 + 0.18 * jax.random.normal(arg_keys[9], (DG,), jnp.float32), 0.1, 1.9)
    mixing = normal_values(arg_keys[10], (LEVELS, LEVELS), LEVELS ** -0.5, 2.0, jnp.float32)
    up_weight = normal_values(arg_keys[11], (DG, FF), DG ** -0.5, 0.25)
    down_weight = normal_values(arg_keys[12], (FF, DG), FF ** -0.5, 0.1875)
    return dict(grid_state=grid_state, observations=observations, destination=destination, subtile=subtile, query_weight=query_weight, key_weight=key_weight, value_weight=value_weight, out_weight=out_weight, sink_logit=sink_logit, norm_gain=norm_gain, mixing=mixing, up_weight=up_weight, down_weight=down_weight)


def attend(queries, token_keys, token_values, valid, sink_logit):

    def per_head(operands):
        q_head, k_head, v_head, sink_head = operands
        scores = jnp.dot(q_head, k_head.T, preferred_element_type=jnp.float32) * (1.0 / math.sqrt(q_head.shape[1]))
        masked = jnp.where(valid, scores, -1e+30)
        peak = jnp.maximum(lax.optimization_barrier(jnp.max(masked, axis=1, keepdims=True)), sink_head)
        weights = jnp.where(valid, jnp.exp(masked - peak), 0.0)
        denominator = jnp.exp(sink_head - peak) + lax.optimization_barrier(jnp.sum(weights, axis=1, keepdims=True))
        probability = (weights / denominator).astype(jnp.bfloat16)
        return jnp.dot(probability, v_head, preferred_element_type=jnp.float32).astype(jnp.bfloat16)
    return lax.map(per_head, (queries, token_keys, token_values, sink_logit))

def split_heads(matrix, head_count):
    return matrix.reshape(matrix.shape[0], head_count, matrix.shape[1] // head_count).transpose(1, 0, 2)

def reference(grid_state, observations, destination, subtile, query_weight, key_weight, value_weight, out_weight, sink_logit, norm_gain, mixing, up_weight, down_weight):
    target = destination[:, 0].astype(jnp.int32)
    tile_ids = jnp.arange(N_TILE, dtype=jnp.int32)
    onehot = (target[:, None] == tile_ids[None, :]).astype(jnp.int32)
    ranking = lax.optimization_barrier(jnp.sum((jnp.cumsum(onehot, axis=0) - onehot) * onehot, axis=1)).astype(jnp.int32)
    slot_index = (target * RECV + ranking).astype(jnp.int32)
    token_bank = jnp.zeros((N_TILE * RECV, DO), observations.dtype).at[slot_index].set(observations)
    slot_codes = jnp.zeros((N_TILE * RECV,), jnp.int32).at[slot_index].set(subtile.astype(jnp.int32) + 1)
    token_bank = token_bank.reshape(N_TILE, RECV, DO)
    slot_codes = slot_codes.reshape(N_TILE, RECV)
    cell_sub = jnp.tile(jnp.arange(CELL_DEV, dtype=jnp.int32) // SUBCELLS, LEVELS)
    grid_tiles = grid_state.reshape(LEVELS, N_TILE, CELL_DEV, DG).transpose(1, 0, 2, 3).reshape(N_TILE, LEVELS * CELL_DEV, DG)

    def per_tile(operands):
        grid_rows, tokens, codes_here = operands
        key_rows = jnp.dot(tokens, key_weight, preferred_element_type=jnp.float32).astype(jnp.bfloat16)
        value_rows = jnp.dot(tokens, value_weight, preferred_element_type=jnp.float32).astype(jnp.bfloat16)
        queries = jnp.dot(grid_rows, query_weight, preferred_element_type=jnp.float32).astype(jnp.bfloat16)
        valid = (codes_here[None, :] > 0) & (jnp.abs(codes_here[None, :] - 1 - cell_sub[:, None]) <= 1)
        head_out = attend(split_heads(queries, HEADS), split_heads(key_rows, HEADS), split_heads(value_rows, HEADS), valid, sink_logit)
        attended = head_out.transpose(1, 0, 2).reshape(grid_rows.shape[0], DG)
        return (grid_rows.astype(jnp.float32) + jnp.dot(attended, out_weight, preferred_element_type=jnp.float32)).astype(jnp.bfloat16)
    updated = lax.map(per_tile, (grid_tiles, token_bank, slot_codes))
    updated = updated.reshape(N_TILE, LEVELS, CELL_DEV, DG).transpose(1, 0, 2, 3).reshape(LEVELS, CELLS, DG)
    wide = updated.astype(jnp.float32)
    inverse = lax.rsqrt(lax.optimization_barrier(jnp.mean(wide * wide, axis=2, keepdims=True)) + 1e-05)
    normed = wide * inverse * norm_gain
    blended = jnp.einsum('lm,mcd->lcd', mixing, normed, precision=lax.Precision.HIGHEST).astype(jnp.bfloat16)
    hidden = jax.nn.gelu(jnp.dot(blended, up_weight, preferred_element_type=jnp.float32)).astype(jnp.bfloat16)
    return (wide + jnp.dot(hidden, down_weight, preferred_element_type=jnp.float32)).astype(jnp.bfloat16)
```

```python
import functools

import jax
import jax.numpy as jnp
from jax import lax
from jax.experimental import pallas as pl
from jax.experimental.pallas import tpu as pltpu
from jax.sharding import PartitionSpec as P

SUBCELLS = 32
HEADS = 8
EMPTY = 64.0
EMPTY_FROM = 48.0
MIB = 1 << 20


def route_kernel(sub_here, target_ref, subtile_ref, tokens_ref, bank_ref, *, tile_count, capacity):
    rows = tokens_ref.shape[0]
    width = tokens_ref.shape[1]
    keep = jnp.abs(subtile_ref[...] - sub_here[0]) <= 1
    target = jnp.where(keep, target_ref[...], -1)
    tile_ids = lax.broadcasted_iota(jnp.int32, (tile_count, rows), 0)
    named = target == tile_ids
    onehot = jnp.where(named, 1.0, 0.0)
    before = lax.broadcasted_iota(jnp.int32, (rows, rows), 0) < lax.broadcasted_iota(
        jnp.int32, (rows, rows), 1
    )
    before = jnp.where(before, 1.0, 0.0).astype(jnp.bfloat16)
    rank = jnp.dot(onehot.astype(jnp.bfloat16), before, preferred_element_type=jnp.float32)
    rank = jnp.where(named, rank, -1.0)
    count = jnp.sum(onehot, axis=1, keepdims=True)
    tokens = tokens_ref[...]
    group = 8
    slot = lax.broadcasted_iota(jnp.int32, (group, capacity, rows), 1).astype(jnp.float32)
    slot_out = lax.broadcasted_iota(jnp.int32, (group, capacity, width), 1).astype(jnp.float32)
    for first in range(0, tile_count, group):
        pick = jnp.where(rank[first : first + group][:, None, :] == slot, 1.0, 0.0)
        pick = pick.reshape(group * capacity, rows).astype(jnp.bfloat16)
        taken = jnp.dot(pick, tokens, preferred_element_type=jnp.float32)
        filled = slot_out < count[first : first + group][:, None, :]
        taken = jnp.where(filled, taken.reshape(group, capacity, width), EMPTY)
        bank_ref[first * capacity : (first + group) * capacity, :] = taken.reshape(
            group * capacity, width
        ).astype(jnp.bfloat16)


def encode_kernel(
    tokens_ref,
    query_ref,
    grid_ref,
    key_weight_ref,
    value_weight_ref,
    out_weight_ref,
    gain_ref,
    up_ref,
    down_ref,
    sink_ref,
    mixing_ref,
    encoded_ref,
    *,
    levels,
):
    rows, width = query_ref.shape
    head_width = width // HEADS
    pair = 2 * head_width
    tokens = tokens_ref[...]
    over_tokens = (((1,), (1,)), ((), ()))
    lane = lax.broadcasted_iota(jnp.int32, (16, tokens.shape[1]), 1)
    first_feature = jnp.where(lane == 0, 1.0, 0.0).astype(jnp.bfloat16)
    marks = lax.dot_general(
        first_feature, tokens, over_tokens, preferred_element_type=jnp.float32
    )[0:1]
    bias = jnp.where(marks > EMPTY_FROM, -1e30, 0.0)
    keys = lax.dot_general(
        key_weight_ref[...], tokens, over_tokens, preferred_element_type=jnp.float32
    ).astype(jnp.bfloat16)
    values = jnp.dot(tokens, value_weight_ref[...], preferred_element_type=jnp.float32).astype(
        jnp.bfloat16
    )
    left = lax.broadcasted_iota(jnp.int32, (rows, pair), 1) < head_width
    attended = []
    for p in range(HEADS // 2):
        lanes = slice(p * pair, (p + 1) * pair)
        query = query_ref[:, lanes].astype(jnp.float32) * head_width**-0.5
        both = jnp.concatenate(
            [jnp.where(left, query, 0.0), jnp.where(left, 0.0, query)], axis=0
        ).astype(jnp.bfloat16)
        scores = jnp.dot(both, keys[lanes], preferred_element_type=jnp.float32) + bias
        row_head = lax.broadcasted_iota(jnp.int32, (2 * rows, 1), 0) < rows
        sink = jnp.where(row_head, sink_ref[2 * p], sink_ref[2 * p + 1])
        peak = jnp.maximum(jnp.max(scores, axis=1, keepdims=True), sink)
        weights = jnp.exp(scores - peak)
        total = jnp.exp(sink - peak) + jnp.sum(weights, axis=1, keepdims=True)
        mixed = jnp.dot(
            weights.astype(jnp.bfloat16), values[:, lanes], preferred_element_type=jnp.float32
        )
        mixed = mixed / total
        attended.append(jnp.where(left, mixed[:rows], mixed[rows:]).astype(jnp.bfloat16))
    attended = jnp.concatenate(attended, axis=1)
    updated = (
        grid_ref[...].astype(jnp.float32)
        + jnp.dot(attended, out_weight_ref[...], preferred_element_type=jnp.float32)
    ).astype(jnp.bfloat16)
    wide = updated.astype(jnp.float32)
    inverse = lax.rsqrt(jnp.mean(wide * wide, axis=1, keepdims=True) + 1e-05)
    normed = wide * inverse * gain_ref[...]
    cells = rows // levels
    parts = [normed[m * cells : (m + 1) * cells] for m in range(levels)]
    blended = []
    for l in range(levels):
        total = mixing_ref[l, 0] * parts[0]
        for m in range(1, levels):
            total = total + mixing_ref[l, m] * parts[m]
        blended.append(total)
    blended = jnp.concatenate(blended, axis=0).astype(jnp.bfloat16)
    hidden = jax.nn.gelu(
        jnp.dot(blended, up_ref[...], preferred_element_type=jnp.float32)
    ).astype(jnp.bfloat16)
    encoded_ref[...] = (
        wide + jnp.dot(hidden, down_ref[...], preferred_element_type=jnp.float32)
    ).astype(jnp.bfloat16)


def body(
    grid_state,
    observations,
    destination,
    subtile,
    query_weight,
    key_weight,
    value_weight,
    out_weight,
    sink_logit,
    norm_gain,
    mixing,
    up_weight,
    down_weight,
):
    tile_count = lax.axis_size("tile")
    levels = lax.axis_size("lev")
    token_rows, token_width = observations.shape
    capacity = 2 * token_rows // tile_count
    cells, width = grid_state.shape[1:]
    cells_here = cells // levels
    rows = levels * cells_here
    sub_here = (lax.axis_index("lev") * cells_here // SUBCELLS).reshape(1)
    smem = pl.BlockSpec(memory_space=pltpu.SMEM)
    vmem = pl.BlockSpec(memory_space=pltpu.VMEM)

    columns = lax.all_to_all(
        grid_state.reshape(levels, cells_here, width), "lev", split_axis=0, concat_axis=0, tiled=True
    ).reshape(rows, width)
    bank = pl.pallas_call(
        functools.partial(route_kernel, tile_count=tile_count, capacity=capacity),
        out_shape=jax.ShapeDtypeStruct((tile_count * capacity, token_width), observations.dtype),
        in_specs=[smem, vmem, vmem, vmem],
        out_specs=vmem,
        compiler_params=pltpu.CompilerParams(vmem_limit_bytes=16 * MIB),
        cost_estimate=pl.CostEstimate(flops=300_000_000, bytes_accessed=MIB, transcendentals=0),
        name="route",
    )(
        sub_here,
        destination.reshape(1, token_rows),
        subtile.reshape(1, token_rows),
        observations,
    )
    received = lax.all_to_all(
        bank.reshape(tile_count, capacity, token_width),
        "tile",
        split_axis=0,
        concat_axis=0,
        tiled=True,
    ).reshape(tile_count * capacity, token_width)
    queries = jnp.dot(columns, query_weight, preferred_element_type=jnp.float32).astype(
        jnp.bfloat16
    )
    encoded = pl.pallas_call(
        functools.partial(encode_kernel, levels=levels),
        out_shape=jax.ShapeDtypeStruct((rows, width), jnp.bfloat16),
        in_specs=[vmem] * 9 + [smem, smem],
        out_specs=vmem,
        compiler_params=pltpu.CompilerParams(vmem_limit_bytes=32 * MIB),
        cost_estimate=pl.CostEstimate(
            flops=1_500_000_000, bytes_accessed=5 * MIB, transcendentals=1_200_000
        ),
        name="encode",
    )(
        received,
        queries,
        columns,
        key_weight.T,
        value_weight,
        out_weight,
        norm_gain.reshape(1, width),
        up_weight,
        down_weight,
        sink_logit,
        mixing,
    )
    return lax.all_to_all(
        encoded.reshape(levels, cells_here, width), "lev", split_axis=0, concat_axis=1, tiled=True
    )


def solution(mesh):
    placed = (
        P("lev", "tile", None),
        P("tile", None),
        P("tile", None),
        P("tile"),
        P(),
        P(),
        P(),
        P(),
        P(),
        P(),
        P(),
        P(),
        P(),
    )
    return jax.shard_map(
        body, mesh=mesh, in_specs=placed, out_specs=P("lev", "tile", None), check_vma=False
    )
```

```python
import functools

import jax
import jax.numpy as jnp
from jax import lax
from jax.experimental import pallas as pl
from jax.experimental.pallas import tpu as pltpu
from jax.sharding import PartitionSpec as P

SUBCELLS = 32
HEADS = 8
EMPTY = 64.0
EMPTY_FROM = 48.0
MIB = 1 << 20


FIRST = 1
LATER = (0, 5, 6, 2)


def pick(pieces, levels):
    return jnp.stack([lax.dynamic_index_in_dim(pieces, l, 0, keepdims=False) for l in levels])


def start_loads(far, near, loaded):
    loads = [pltpu.make_async_copy(f, n, loaded.at[i]) for i, (f, n) in enumerate(zip(far, near))]
    for load in loads:
        load.start()
    return loads


def route_kernel(
    sub_here,
    target_hbm,
    subtile_hbm,
    tokens_hbm,
    bank_ref,
    target_ref,
    subtile_ref,
    tokens_ref,
    loaded,
    *,
    tile_count,
    capacity,
):
    loads = start_loads(
        (target_hbm, subtile_hbm, tokens_hbm), (target_ref, subtile_ref, tokens_ref), loaded
    )
    rows = tokens_ref.shape[0]
    width = tokens_ref.shape[1]
    before = lax.broadcasted_iota(jnp.int32, (rows, rows), 0) < lax.broadcasted_iota(
        jnp.int32, (rows, rows), 1
    )
    before = jnp.where(before, 1.0, 0.0).astype(jnp.bfloat16)
    loads[0].wait()
    loads[1].wait()
    keep = jnp.abs(subtile_ref[...] - sub_here[0]) <= 1
    target = jnp.where(keep, target_ref[...], -1)
    tile_ids = lax.broadcasted_iota(jnp.int32, (tile_count, rows), 0)
    named = target == tile_ids
    onehot = jnp.where(named, 1.0, 0.0)
    rank = jnp.dot(onehot.astype(jnp.bfloat16), before, preferred_element_type=jnp.float32)
    rank = jnp.where(named, rank, -1.0)
    count = jnp.sum(onehot, axis=1, keepdims=True)
    loads[2].wait()
    tokens = tokens_ref[...]
    group = 8
    slot = lax.broadcasted_iota(jnp.int32, (group, capacity, rows), 1).astype(jnp.float32)
    slot_out = lax.broadcasted_iota(jnp.int32, (group, capacity, width), 1).astype(jnp.float32)
    for first in range(0, tile_count, group):
        pick = jnp.where(rank[first : first + group][:, None, :] == slot, 1.0, 0.0)
        pick = pick.reshape(group * capacity, rows).astype(jnp.bfloat16)
        taken = jnp.dot(pick, tokens, preferred_element_type=jnp.float32)
        filled = slot_out < count[first : first + group][:, None, :]
        taken = jnp.where(filled, taken.reshape(group, capacity, width), EMPTY)
        bank_ref[first * capacity : (first + group) * capacity, :] = taken.reshape(
            group * capacity, width
        ).astype(jnp.bfloat16)


def stage_kernel(key_ref, key_columns_ref):
    key_columns_ref[...] = key_ref[...].astype(jnp.float32).T.astype(jnp.bfloat16)


def query_kernel(*refs):
    *piece_refs, weight_ref, columns_ref, query_ref = refs
    columns = jnp.concatenate([ref[...] for ref in piece_refs], axis=0)
    columns_ref[...] = columns
    query = jnp.dot(columns, weight_ref[...], preferred_element_type=jnp.float32)
    query_ref[...] = query.astype(jnp.bfloat16)


def encode_kernel(*refs, block_order):
    level_here, tokens_ref, key_weight_ref, query_ref, grid_ref = refs[:5]
    far, encoded_ref, near, loaded = refs[5:12], refs[12], refs[13:20], refs[20]
    (
        value_weight_ref,
        sink_ref,
        out_weight_ref,
        gain_ref,
        mixing_ref,
        up_ref,
        down_ref,
    ) = near
    loads = start_loads(far, near, loaded)
    levels = len(block_order)
    rows, width = query_ref.shape
    head_width = width // HEADS
    pair = 2 * head_width
    tokens = tokens_ref[...]
    over_tokens = (((1,), (1,)), ((), ()))
    lane = lax.broadcasted_iota(jnp.int32, (16, tokens.shape[1]), 1)
    first_feature = jnp.where(lane == 0, 1.0, 0.0).astype(jnp.bfloat16)
    marks = lax.dot_general(
        first_feature, tokens, over_tokens, preferred_element_type=jnp.float32
    )[0:1]
    bias = jnp.where(marks > EMPTY_FROM, -1e30, 0.0)
    keys = lax.dot_general(
        key_weight_ref[...], tokens, over_tokens, preferred_element_type=jnp.float32
    ).astype(jnp.bfloat16)
    loads[0].wait()
    loads[1].wait()
    values = jnp.dot(tokens, value_weight_ref[...], preferred_element_type=jnp.float32).astype(
        jnp.bfloat16
    )
    left = lax.broadcasted_iota(jnp.int32, (rows, pair), 1) < head_width
    attended = []
    for p in range(HEADS // 2):
        lanes = slice(p * pair, (p + 1) * pair)
        query = query_ref[:, lanes].astype(jnp.float32) * head_width**-0.5
        both = jnp.concatenate(
            [jnp.where(left, query, 0.0), jnp.where(left, 0.0, query)], axis=0
        ).astype(jnp.bfloat16)
        scores = jnp.dot(both, keys[lanes], preferred_element_type=jnp.float32) + bias
        row_head = lax.broadcasted_iota(jnp.int32, (2 * rows, 1), 0) < rows
        sink = jnp.where(row_head, sink_ref[2 * p], sink_ref[2 * p + 1])
        peak = jnp.maximum(jnp.max(scores, axis=1, keepdims=True), sink)
        weights = jnp.exp(scores - peak)
        total = jnp.exp(sink - peak) + jnp.sum(weights, axis=1, keepdims=True)
        mixed = jnp.dot(
            weights.astype(jnp.bfloat16), values[:, lanes], preferred_element_type=jnp.float32
        )
        mixed = mixed / total
        attended.append(jnp.where(left, mixed[:rows], mixed[rows:]).astype(jnp.bfloat16))
    attended = jnp.concatenate(attended, axis=1)
    for load in loads[2:5]:
        load.wait()
    updated = (
        grid_ref[...].astype(jnp.float32)
        + jnp.dot(attended, out_weight_ref[...], preferred_element_type=jnp.float32)
    ).astype(jnp.bfloat16)
    wide = updated.astype(jnp.float32)
    inverse = lax.rsqrt(jnp.mean(wide * wide, axis=1, keepdims=True) + 1e-05)
    normed = wide * inverse * gain_ref[...]
    cells = rows // levels
    parts = [normed[m * cells : (m + 1) * cells] for m in range(levels)]
    held = [level_here[0] ^ offset for offset in block_order]
    blended = []
    for l in held:
        total = mixing_ref[l, held[0]] * parts[0]
        for m in range(1, levels):
            total = total + mixing_ref[l, held[m]] * parts[m]
        blended.append(total)
    blended = jnp.concatenate(blended, axis=0).astype(jnp.bfloat16)
    loads[5].wait()
    hidden = jax.nn.gelu(
        jnp.dot(blended, up_ref[...], preferred_element_type=jnp.float32)
    ).astype(jnp.bfloat16)
    loads[6].wait()
    encoded = (
        wide + jnp.dot(hidden, down_ref[...], preferred_element_type=jnp.float32)
    ).astype(jnp.bfloat16)
    for e, l in enumerate(held):
        start = pl.multiple_of(l * cells, cells)
        encoded_ref[pl.ds(start, cells), :] = encoded[e * cells : (e + 1) * cells]


def exchange_permute(array, offset, count):
    return lax.ppermute(array, "lev", [(i, i ^ offset) for i in range(count)])


def body(
    grid_state,
    observations,
    destination,
    subtile,
    query_weight,
    key_weight,
    value_weight,
    out_weight,
    sink_logit,
    norm_gain,
    mixing,
    up_weight,
    down_weight,
):
    tile_count = lax.axis_size("tile")
    levels = lax.axis_size("lev")
    token_rows, token_width = observations.shape
    capacity = 2 * token_rows // tile_count
    cells, width = grid_state.shape[1:]
    cells_here = cells // levels
    rows = levels * cells_here
    sub_here = (lax.axis_index("lev") * cells_here // SUBCELLS).reshape(1)
    smem = pl.BlockSpec(memory_space=pltpu.SMEM)
    vmem = pl.BlockSpec(memory_space=pltpu.VMEM)
    far = pl.BlockSpec(memory_space=pl.ANY)

    here = lax.axis_index("lev")
    pieces = grid_state.reshape(levels, cells_here, width)
    came = exchange_permute(pick(pieces, [here ^ FIRST ^ o for o in LATER]), FIRST, levels)
    bank = pl.pallas_call(
        functools.partial(route_kernel, tile_count=tile_count, capacity=capacity),
        out_shape=jax.ShapeDtypeStruct((tile_count * capacity, token_width), observations.dtype),
        in_specs=[smem, far, far, far],
        out_specs=vmem,
        scratch_shapes=[
            pltpu.VMEM((1, token_rows), jnp.int32),
            pltpu.VMEM((1, token_rows), jnp.int32),
            pltpu.VMEM(observations.shape, observations.dtype),
            pltpu.SemaphoreType.DMA((3,)),
        ],
        compiler_params=pltpu.CompilerParams(vmem_limit_bytes=32 * MIB),
        cost_estimate=pl.CostEstimate(flops=300_000_000, bytes_accessed=MIB, transcendentals=0),
        name="route",
    )(
        sub_here,
        *(
            pltpu.with_memory_space_constraint(o, pltpu.HBM)
            for o in (
                destination.reshape(1, token_rows),
                subtile.reshape(1, token_rows),
                observations,
            )
        ),
    )
    bank, came = lax.optimization_barrier((bank, came))
    received = lax.all_to_all(
        bank.reshape(tile_count, capacity, token_width),
        "tile",
        split_axis=0,
        concat_axis=0,
        tiled=True,
    ).reshape(tile_count * capacity, token_width)
    key_columns = pl.pallas_call(
        stage_kernel,
        out_shape=jax.ShapeDtypeStruct(key_weight.shape[::-1], key_weight.dtype),
        in_specs=[vmem],
        out_specs=vmem,
        compiler_params=pltpu.CompilerParams(vmem_limit_bytes=8 * MIB),
        cost_estimate=pl.CostEstimate(flops=1000, bytes_accessed=MIB, transcendentals=0),
        name="stage",
    )(key_weight)
    parts = []
    for came_block, offset in zip(came, LATER):
        both = jnp.stack([pick(pieces, [here ^ offset])[0], came_block])
        both = both.reshape(2 * cells_here, width)
        parts.append(both if offset == 0 else exchange_permute(both, offset, levels))
    columns, queries = pl.pallas_call(
        query_kernel,
        out_shape=[jax.ShapeDtypeStruct((rows, width), jnp.bfloat16)] * 2,
        in_specs=[vmem] * (len(parts) + 1),
        out_specs=[vmem] * 2,
        compiler_params=pltpu.CompilerParams(vmem_limit_bytes=8 * MIB),
        cost_estimate=pl.CostEstimate(flops=67_000_000, bytes_accessed=MIB, transcendentals=0),
        name="query",
    )(*parts, query_weight)
    operands = [
        value_weight,
        sink_logit,
        out_weight,
        norm_gain.reshape(1, width),
        mixing,
        up_weight,
        down_weight,
    ]
    operands = [pltpu.with_memory_space_constraint(o, pltpu.HBM) for o in operands]
    encoded = pl.pallas_call(
        functools.partial(
            encode_kernel, block_order=[o ^ first for o in LATER for first in (0, FIRST)]
        ),
        out_shape=jax.ShapeDtypeStruct((rows, width), jnp.bfloat16),
        in_specs=[smem] + [vmem] * 4 + [far] * len(operands),
        out_specs=vmem,
        scratch_shapes=[
            (pltpu.SMEM if operand.shape[-1] == HEADS else pltpu.VMEM)(operand.shape, operand.dtype)
            for operand in operands
        ]
        + [pltpu.SemaphoreType.DMA((len(operands),))],
        compiler_params=pltpu.CompilerParams(vmem_limit_bytes=32 * MIB),
        cost_estimate=pl.CostEstimate(
            flops=1_500_000_000, bytes_accessed=5 * MIB, transcendentals=1_200_000
        ),
        name="encode",
    )(here.reshape(1), received, key_columns, queries, columns, *operands)
    return lax.all_to_all(
        encoded.reshape(levels, cells_here, width), "lev", split_axis=0, concat_axis=1, tiled=True
    )


def solution(mesh):
    placed = (
        P("lev", "tile", None),
        P("tile", None),
        P("tile", None),
        P("tile"),
        P(),
        P(),
        P(),
        P(),
        P(),
        P(),
        P(),
        P(),
        P(),
    )
    return jax.shard_map(
        body, mesh=mesh, in_specs=placed, out_specs=P("lev", "tile", None), check_vma=False
    )
```

```python
import functools

import jax
import jax.numpy as jnp
from jax import lax
from jax.experimental import pallas as pl
from jax.experimental.pallas import tpu as pltpu
from jax.sharding import PartitionSpec as P

SUBCELLS = 32
HEADS = 8
EMPTY = 64.0
EMPTY_FROM = 48.0
MIB = 1 << 20


FIRST = 1
LATER = (0, 5, 6, 2)


def pick(pieces, levels):
    return jnp.stack([lax.dynamic_index_in_dim(pieces, l, 0, keepdims=False) for l in levels])


def start_loads(far, near, loaded):
    loads = [pltpu.make_async_copy(f, n, loaded.at[i]) for i, (f, n) in enumerate(zip(far, near))]
    for load in loads:
        load.start()
    return loads


def fetch_kernel(
    level_here,
    pieces_hbm,
    target_hbm,
    subtile_hbm,
    tokens_hbm,
    half_ref,
    target_ref,
    subtile_ref,
    tokens_ref,
    loaded,
):
    far = [target_hbm, subtile_hbm, tokens_hbm]
    near = [target_ref, subtile_ref, tokens_ref]
    for i, offset in enumerate(LATER):
        far.append(pieces_hbm.at[level_here[0] ^ FIRST ^ offset])
        near.append(half_ref.at[i])
    for load in start_loads(far, near, loaded):
        load.wait()


def route_kernel(
    sub_here,
    target_ref,
    subtile_ref,
    tokens_ref,
    bank_ref,
    *,
    tile_count,
    capacity,
):
    rows = tokens_ref.shape[0]
    width = tokens_ref.shape[1]
    before = lax.broadcasted_iota(jnp.int32, (rows, rows), 0) < lax.broadcasted_iota(
        jnp.int32, (rows, rows), 1
    )
    before = jnp.where(before, 1.0, 0.0).astype(jnp.bfloat16)
    keep = jnp.abs(subtile_ref[...] - sub_here[0]) <= 1
    target = jnp.where(keep, target_ref[...], -1)
    tile_ids = lax.broadcasted_iota(jnp.int32, (tile_count, rows), 0)
    named = target == tile_ids
    onehot = jnp.where(named, 1.0, 0.0)
    rank = jnp.dot(onehot.astype(jnp.bfloat16), before, preferred_element_type=jnp.float32)
    rank = jnp.where(named, rank, -1.0)
    count = jnp.sum(onehot, axis=1, keepdims=True)
    tokens = tokens_ref[...]
    group = 8
    slot = lax.broadcasted_iota(jnp.int32, (group, capacity, rows), 1).astype(jnp.float32)
    slot_out = lax.broadcasted_iota(jnp.int32, (group, capacity, width), 1).astype(jnp.float32)
    for first in range(0, tile_count, group):
        pick = jnp.where(rank[first : first + group][:, None, :] == slot, 1.0, 0.0)
        pick = pick.reshape(group * capacity, rows).astype(jnp.bfloat16)
        taken = jnp.dot(pick, tokens, preferred_element_type=jnp.float32)
        filled = slot_out < count[first : first + group][:, None, :]
        taken = jnp.where(filled, taken.reshape(group, capacity, width), EMPTY)
        bank_ref[first * capacity : (first + group) * capacity, :] = taken.reshape(
            group * capacity, width
        ).astype(jnp.bfloat16)


def query_kernel(*refs):
    *piece_refs, weight_ref, columns_ref, query_ref = refs
    columns = jnp.concatenate([ref[...] for ref in piece_refs], axis=0)
    columns_ref[...] = columns
    query = jnp.dot(columns, weight_ref[...], preferred_element_type=jnp.float32)
    query_ref[...] = query.astype(jnp.bfloat16)


def encode_kernel(*refs, block_order):
    (
        level_here,
        tokens_ref,
        key_weight_ref,
        value_weight_ref,
        out_weight_ref,
        query_ref,
        grid_ref,
    ) = refs[:7]
    far, encoded_ref, near, loaded = refs[7:12], refs[12], refs[13:18], refs[18]
    sink_ref, gain_ref, mixing_ref, up_ref, down_ref = near
    loads = start_loads(far, near, loaded)
    levels = len(block_order)
    rows, width = query_ref.shape
    head_width = width // HEADS
    tokens = tokens_ref[...]
    over_tokens = (((1,), (1,)), ((), ()))
    lane = lax.broadcasted_iota(jnp.int32, (16, tokens.shape[1]), 1)
    first_feature = jnp.where(lane == 0, 1.0, 0.0).astype(jnp.bfloat16)
    marks = lax.dot_general(
        first_feature, tokens, over_tokens, preferred_element_type=jnp.float32
    )[0:1]
    bias = jnp.where(marks > EMPTY_FROM, -1e30, 0.0)
    keys = jnp.dot(tokens, key_weight_ref[...], preferred_element_type=jnp.float32).astype(
        jnp.bfloat16
    )
    values = jnp.dot(tokens, value_weight_ref[...], preferred_element_type=jnp.float32).astype(
        jnp.bfloat16
    )
    group = 2 * head_width
    lane_head = lax.broadcasted_iota(jnp.int32, (rows, group), 1) // head_width
    loads[0].wait()
    attended = []
    for p in range(HEADS // 2):
        lanes = slice(p * group, (p + 1) * group)
        query = query_ref[:, lanes].astype(jnp.float32) * head_width**-0.5
        value = values[:, lanes]
        value = jnp.concatenate([value, jnp.ones_like(value)], axis=1)
        mine = None
        for h in range(2):
            sink = sink_ref[2 * p + h]
            one = jnp.where(lane_head == h, query, 0.0).astype(jnp.bfloat16)
            scores = bias + lax.dot_general(
                one, keys[:, lanes], over_tokens, preferred_element_type=jnp.float32
            )
            peak = jnp.maximum(jnp.max(scores, axis=1, keepdims=True), sink)
            weights = jnp.exp(scores - peak)
            mixed = jnp.dot(weights.astype(jnp.bfloat16), value, preferred_element_type=jnp.float32)
            mixed = mixed[:, :group] / (mixed[:, group:] + jnp.exp(sink - peak))
            mine = mixed if mine is None else jnp.where(lane_head == h, mixed, mine)
        attended.append(mine.astype(jnp.bfloat16))
    attended = jnp.concatenate(attended, axis=1)
    updated = (
        grid_ref[...].astype(jnp.float32)
        + jnp.dot(attended, out_weight_ref[...], preferred_element_type=jnp.float32)
    ).astype(jnp.bfloat16)
    wide = updated.astype(jnp.float32)
    loads[1].wait()
    loads[2].wait()
    inverse = lax.rsqrt(jnp.mean(wide * wide, axis=1, keepdims=True) + 1e-05)
    normed = wide * inverse * gain_ref[...]
    cells = rows // levels
    parts = [normed[m * cells : (m + 1) * cells] for m in range(levels)]
    held = [level_here[0] ^ offset for offset in block_order]
    blended = []
    for l in held:
        total = mixing_ref[l, held[0]] * parts[0]
        for m in range(1, levels):
            total = total + mixing_ref[l, held[m]] * parts[m]
        blended.append(total)
    blended = jnp.concatenate(blended, axis=0).astype(jnp.bfloat16)
    loads[3].wait()
    hidden = jax.nn.gelu(
        jnp.dot(blended, up_ref[...], preferred_element_type=jnp.float32)
    ).astype(jnp.bfloat16)
    loads[4].wait()
    encoded = (
        wide + jnp.dot(hidden, down_ref[...], preferred_element_type=jnp.float32)
    ).astype(jnp.bfloat16)
    for e, l in enumerate(held):
        start = pl.multiple_of(l * cells, cells)
        encoded_ref[pl.ds(start, cells), :] = encoded[e * cells : (e + 1) * cells]


def exchange_permute(array, offset, count):
    return lax.ppermute(array, "lev", [(i, i ^ offset) for i in range(count)])


def body(
    grid_state,
    observations,
    destination,
    subtile,
    query_weight,
    key_weight,
    value_weight,
    out_weight,
    sink_logit,
    norm_gain,
    mixing,
    up_weight,
    down_weight,
):
    tile_count = lax.axis_size("tile")
    levels = lax.axis_size("lev")
    token_rows, token_width = observations.shape
    capacity = 2 * token_rows // tile_count
    cells, width = grid_state.shape[1:]
    cells_here = cells // levels
    rows = levels * cells_here
    sub_here = (lax.axis_index("lev") * cells_here // SUBCELLS).reshape(1)
    smem = pl.BlockSpec(memory_space=pltpu.SMEM)
    vmem = pl.BlockSpec(memory_space=pltpu.VMEM)
    far = pl.BlockSpec(memory_space=pl.ANY)

    here = lax.axis_index("lev")
    pieces = grid_state.reshape(levels, cells_here, width)
    half, target, subtile_row, tokens = pl.pallas_call(
        fetch_kernel,
        out_shape=[
            pltpu.VMEM((len(LATER), cells_here, width), grid_state.dtype),
            pltpu.VMEM((1, token_rows), jnp.int32),
            pltpu.VMEM((1, token_rows), jnp.int32),
            pltpu.VMEM(observations.shape, observations.dtype),
        ],
        in_specs=[smem] + [far] * 4,
        out_specs=[vmem] * 4,
        scratch_shapes=[pltpu.SemaphoreType.DMA((3 + len(LATER),))],
        compiler_params=pltpu.CompilerParams(vmem_limit_bytes=8 * MIB),
        cost_estimate=pl.CostEstimate(flops=1000, bytes_accessed=MIB, transcendentals=0),
        name="fetch",
    )(
        here.reshape(1),
        *(
            pltpu.with_memory_space_constraint(o, pltpu.HBM)
            for o in (
                pieces,
                destination.reshape(1, token_rows),
                subtile.reshape(1, token_rows),
                observations,
            )
        ),
    )
    came = exchange_permute(half, FIRST, levels)
    bank = pl.pallas_call(
        functools.partial(route_kernel, tile_count=tile_count, capacity=capacity),
        out_shape=jax.ShapeDtypeStruct((tile_count * capacity, token_width), observations.dtype),
        in_specs=[smem] + [vmem] * 3,
        out_specs=vmem,
        compiler_params=pltpu.CompilerParams(vmem_limit_bytes=32 * MIB),
        cost_estimate=pl.CostEstimate(flops=300_000_000, bytes_accessed=MIB, transcendentals=0),
        name="route",
    )(sub_here, target, subtile_row, tokens)
    bank, came = lax.optimization_barrier((bank, came))
    received = lax.all_to_all(
        bank.reshape(tile_count, capacity, token_width),
        "tile",
        split_axis=0,
        concat_axis=0,
        tiled=True,
    ).reshape(tile_count * capacity, token_width)
    parts = []
    for came_block, offset in zip(came, LATER):
        both = jnp.stack([pick(pieces, [here ^ offset])[0], came_block])
        both = both.reshape(2 * cells_here, width)
        parts.append(both if offset == 0 else exchange_permute(both, offset, levels))
    columns, queries = pl.pallas_call(
        query_kernel,
        out_shape=[jax.ShapeDtypeStruct((rows, width), jnp.bfloat16)] * 2,
        in_specs=[vmem] * (len(parts) + 1),
        out_specs=[vmem] * 2,
        compiler_params=pltpu.CompilerParams(vmem_limit_bytes=8 * MIB),
        cost_estimate=pl.CostEstimate(flops=67_000_000, bytes_accessed=MIB, transcendentals=0),
        name="query",
    )(*parts, query_weight)
    operands = [
        sink_logit,
        norm_gain.reshape(1, width),
        mixing,
        up_weight,
        down_weight,
    ]
    operands = [pltpu.with_memory_space_constraint(o, pltpu.HBM) for o in operands]
    encoded = pl.pallas_call(
        functools.partial(
            encode_kernel, block_order=[o ^ first for o in LATER for first in (0, FIRST)]
        ),
        out_shape=jax.ShapeDtypeStruct((rows, width), jnp.bfloat16),
        in_specs=[smem] + [vmem] * 6 + [far] * len(operands),
        out_specs=vmem,
        scratch_shapes=[
            (pltpu.SMEM if operand.shape[-1] == HEADS else pltpu.VMEM)(operand.shape, operand.dtype)
            for operand in operands
        ]
        + [pltpu.SemaphoreType.DMA((len(operands),))],
        compiler_params=pltpu.CompilerParams(vmem_limit_bytes=32 * MIB),
        cost_estimate=pl.CostEstimate(
            flops=1_500_000_000, bytes_accessed=5 * MIB, transcendentals=1_200_000
        ),
        name="encode",
    )(here.reshape(1), received, key_weight, value_weight, out_weight, queries, columns, *operands)
    return lax.all_to_all(
        encoded.reshape(levels, cells_here, width), "lev", split_axis=0, concat_axis=1, tiled=True
    )


def solution(mesh):
    placed = (
        P("lev", "tile", None),
        P("tile", None),
        P("tile", None),
        P("tile"),
        P(),
        P(),
        P(),
        P(),
        P(),
        P(),
        P(),
        P(),
        P(),
    )
    return jax.shard_map(
        body, mesh=mesh, in_specs=placed, out_specs=P("lev", "tile", None), check_vma=False
    )
```

```python
import functools

import jax
import jax.numpy as jnp
from jax import lax
from jax.experimental import pallas as pl
from jax.experimental.pallas import tpu as pltpu
from jax.sharding import PartitionSpec as P

SUBCELLS = 32
HEADS = 8
EMPTY = 64.0
EMPTY_FROM = 48.0
MIB = 1 << 20


FIRST = 1
LATER = (0, 2, 6, 5)


def pick(pieces, levels):
    return jnp.stack([lax.dynamic_index_in_dim(pieces, l, 0, keepdims=False) for l in levels])


def start_loads(far, near, loaded):
    loads = [pltpu.make_async_copy(f, n, loaded.at[i]) for i, (f, n) in enumerate(zip(far, near))]
    for load in loads:
        load.start()
    return loads


def fetch_kernel(
    level_here,
    pieces_hbm,
    target_hbm,
    subtile_hbm,
    tokens_hbm,
    half_ref,
    target_ref,
    subtile_ref,
    tokens_ref,
    loaded,
):
    far = [target_hbm, subtile_hbm, tokens_hbm]
    near = [target_ref, subtile_ref, tokens_ref]
    for i, offset in enumerate(LATER):
        far.append(pieces_hbm.at[level_here[0] ^ FIRST ^ offset])
        near.append(half_ref.at[i])
    for load in start_loads(far, near, loaded):
        load.wait()


def route_kernel(
    sub_here,
    target_ref,
    subtile_ref,
    tokens_ref,
    bank_ref,
    *spare_ref,
    tile_count,
    capacity,
):
    for ref in spare_ref:
        ref[...] = jnp.zeros(ref.shape, ref.dtype)
    rows = tokens_ref.shape[0]
    width = tokens_ref.shape[1]
    before = lax.broadcasted_iota(jnp.int32, (rows, rows), 0) < lax.broadcasted_iota(
        jnp.int32, (rows, rows), 1
    )
    before = jnp.where(before, 1.0, 0.0).astype(jnp.bfloat16)
    keep = jnp.abs(subtile_ref[...] - sub_here[0]) <= 1
    target = jnp.where(keep, target_ref[...], -1)
    tile_ids = lax.broadcasted_iota(jnp.int32, (tile_count, rows), 0)
    named = target == tile_ids
    onehot = jnp.where(named, 1.0, 0.0)
    rank = jnp.dot(onehot.astype(jnp.bfloat16), before, preferred_element_type=jnp.float32)
    rank = jnp.where(named, rank, -1.0)
    count = jnp.sum(onehot, axis=1, keepdims=True)
    tokens = tokens_ref[...]
    group = 8
    slot = lax.broadcasted_iota(jnp.int32, (group, capacity, rows), 1).astype(jnp.float32)
    slot_out = lax.broadcasted_iota(jnp.int32, (group, capacity, width), 1).astype(jnp.float32)
    for first in range(0, tile_count, group):
        pick = jnp.where(rank[first : first + group][:, None, :] == slot, 1.0, 0.0)
        pick = pick.reshape(group * capacity, rows).astype(jnp.bfloat16)
        taken = jnp.dot(pick, tokens, preferred_element_type=jnp.float32)
        filled = slot_out < count[first : first + group][:, None, :]
        taken = jnp.where(filled, taken.reshape(group, capacity, width), EMPTY)
        bank_ref[first * capacity : (first + group) * capacity, :] = taken.reshape(
            group * capacity, width
        ).astype(jnp.bfloat16)


def query_kernel(*refs):
    *piece_refs, weight_ref, columns_ref, query_ref = refs
    columns = jnp.concatenate([ref[...] for ref in piece_refs], axis=0)
    columns_ref[...] = columns
    query = jnp.dot(columns, weight_ref[...], preferred_element_type=jnp.float32)
    query_ref[...] = query.astype(jnp.bfloat16)


def encode_kernel(*refs, block_order):
    (
        level_here,
        tokens_ref,
        key_weight_ref,
        value_weight_ref,
        out_weight_ref,
        query_ref,
        grid_ref,
    ) = refs[:7]
    far, encoded_ref, near, loaded = refs[7:12], refs[12], refs[13:18], refs[18]
    sink_ref, gain_ref, mixing_ref, up_ref, down_ref = near
    loads = start_loads(far, near, loaded)
    levels = len(block_order)
    rows, width = query_ref.shape
    head_width = width // HEADS
    tokens = tokens_ref[...]
    over_tokens = (((1,), (1,)), ((), ()))
    lane = lax.broadcasted_iota(jnp.int32, (16, tokens.shape[1]), 1)
    first_feature = jnp.where(lane == 0, 1.0, 0.0).astype(jnp.bfloat16)
    marks = lax.dot_general(
        first_feature, tokens, over_tokens, preferred_element_type=jnp.float32
    )[0:1]
    bias = jnp.where(marks > EMPTY_FROM, -1e30, 0.0)
    keys = jnp.dot(tokens, key_weight_ref[...], preferred_element_type=jnp.float32).astype(
        jnp.bfloat16
    )
    values = jnp.dot(tokens, value_weight_ref[...], preferred_element_type=jnp.float32).astype(
        jnp.bfloat16
    )
    group = 2 * head_width
    lane_head = lax.broadcasted_iota(jnp.int32, (rows, group), 1) // head_width
    loads[0].wait()
    attended = []
    for p in range(HEADS // 2):
        lanes = slice(p * group, (p + 1) * group)
        query = query_ref[:, lanes].astype(jnp.float32) * head_width**-0.5
        value = values[:, lanes]
        value = jnp.concatenate([value, jnp.ones_like(value)], axis=1)
        mine = None
        for h in range(2):
            sink = sink_ref[2 * p + h]
            one = jnp.where(lane_head == h, query, 0.0).astype(jnp.bfloat16)
            scores = bias + lax.dot_general(
                one, keys[:, lanes], over_tokens, preferred_element_type=jnp.float32
            )
            peak = jnp.maximum(jnp.max(scores, axis=1, keepdims=True), sink)
            weights = jnp.exp(scores - peak)
            mixed = jnp.dot(weights.astype(jnp.bfloat16), value, preferred_element_type=jnp.float32)
            mixed = mixed[:, :group] / (mixed[:, group:] + jnp.exp(sink - peak))
            mine = mixed if mine is None else jnp.where(lane_head == h, mixed, mine)
        attended.append(mine.astype(jnp.bfloat16))
    attended = jnp.concatenate(attended, axis=1)
    updated = (
        grid_ref[...].astype(jnp.float32)
        + jnp.dot(attended, out_weight_ref[...], preferred_element_type=jnp.float32)
    ).astype(jnp.bfloat16)
    wide = updated.astype(jnp.float32)
    loads[1].wait()
    loads[2].wait()
    inverse = lax.rsqrt(jnp.mean(wide * wide, axis=1, keepdims=True) + 1e-05)
    normed = wide * inverse * gain_ref[...]
    cells = rows // levels
    parts = [normed[m * cells : (m + 1) * cells] for m in range(levels)]
    held = [level_here[0] ^ offset for offset in block_order]
    blended = []
    for l in held:
        total = mixing_ref[l, held[0]] * parts[0]
        for m in range(1, levels):
            total = total + mixing_ref[l, held[m]] * parts[m]
        blended.append(total)
    blended = jnp.concatenate(blended, axis=0).astype(jnp.bfloat16)
    loads[3].wait()
    hidden = jax.nn.gelu(
        jnp.dot(blended, up_ref[...], preferred_element_type=jnp.float32)
    ).astype(jnp.bfloat16)
    loads[4].wait()
    encoded = (
        wide + jnp.dot(hidden, down_ref[...], preferred_element_type=jnp.float32)
    ).astype(jnp.bfloat16)
    for e, l in enumerate(held):
        start = pl.multiple_of(l * cells, cells)
        encoded_ref[pl.ds(start, cells), :] = encoded[e * cells : (e + 1) * cells]


def exchange_permute(array, offset, count):
    return lax.ppermute(array, "lev", [(i, i ^ offset) for i in range(count)])


def body(
    grid_state,
    observations,
    destination,
    subtile,
    query_weight,
    key_weight,
    value_weight,
    out_weight,
    sink_logit,
    norm_gain,
    mixing,
    up_weight,
    down_weight,
):
    tile_count = lax.axis_size("tile")
    levels = lax.axis_size("lev")
    token_rows, token_width = observations.shape
    capacity = 2 * token_rows // tile_count
    cells, width = grid_state.shape[1:]
    cells_here = cells // levels
    rows = levels * cells_here
    sub_here = (lax.axis_index("lev") * cells_here // SUBCELLS).reshape(1)
    smem = pl.BlockSpec(memory_space=pltpu.SMEM)
    vmem = pl.BlockSpec(memory_space=pltpu.VMEM)
    far = pl.BlockSpec(memory_space=pl.ANY)

    here = lax.axis_index("lev")
    pieces = grid_state.reshape(levels, cells_here, width)
    half, target, subtile_row, tokens = pl.pallas_call(
        fetch_kernel,
        out_shape=[
            pltpu.VMEM((len(LATER), cells_here, width), grid_state.dtype),
            pltpu.VMEM((1, token_rows), jnp.int32),
            pltpu.VMEM((1, token_rows), jnp.int32),
            pltpu.VMEM(observations.shape, observations.dtype),
        ],
        in_specs=[smem] + [far] * 4,
        out_specs=[vmem] * 4,
        scratch_shapes=[pltpu.SemaphoreType.DMA((3 + len(LATER),))],
        compiler_params=pltpu.CompilerParams(vmem_limit_bytes=8 * MIB),
        cost_estimate=pl.CostEstimate(flops=1000, bytes_accessed=MIB, transcendentals=0),
        name="fetch",
    )(
        here.reshape(1),
        *(
            pltpu.with_memory_space_constraint(o, pltpu.HBM)
            for o in (
                pieces,
                destination.reshape(1, token_rows),
                subtile.reshape(1, token_rows),
                observations,
            )
        ),
    )
    bank_shape = jax.ShapeDtypeStruct((tile_count * capacity, token_width), observations.dtype)
    half_shape = jax.ShapeDtypeStruct(half.shape, half.dtype)

    def route(out_shape):
        return pl.pallas_call(
            functools.partial(route_kernel, tile_count=tile_count, capacity=capacity),
            out_shape=out_shape,
            in_specs=[smem] + [vmem] * 3,
            out_specs=[vmem] * len(out_shape),
            compiler_params=pltpu.CompilerParams(vmem_limit_bytes=32 * MIB),
            cost_estimate=pl.CostEstimate(
                flops=300_000_000, bytes_accessed=MIB, transcendentals=0
            ),
            name="route",
        )

    early = (lax.axis_index("tile") // 2) % 8 < 3
    bank, came = lax.cond(
        early,
        lambda h, *of: (route([bank_shape])(*of)[0], exchange_permute(h, FIRST, levels)),
        lambda h, *of: tuple(route([bank_shape, half_shape])(*of)),
        half,
        sub_here,
        target,
        subtile_row,
        tokens,
    )
    bank, came = lax.optimization_barrier((bank, came))
    received = lax.all_to_all(
        bank.reshape(tile_count, capacity, token_width),
        "tile",
        split_axis=0,
        concat_axis=0,
        tiled=True,
    ).reshape(tile_count * capacity, token_width)
    came_late = lax.cond(
        early, jnp.zeros_like, lambda h: exchange_permute(h, FIRST, levels), half
    )
    came = jnp.where(early, came, came_late)
    parts = []
    for came_block, offset in zip(came, LATER):
        both = jnp.stack([pick(pieces, [here ^ offset])[0], came_block])
        both = both.reshape(2 * cells_here, width)
        parts.append(both if offset == 0 else exchange_permute(both, offset, levels))
    columns, queries = pl.pallas_call(
        query_kernel,
        out_shape=[jax.ShapeDtypeStruct((rows, width), jnp.bfloat16)] * 2,
        in_specs=[vmem] * (len(parts) + 1),
        out_specs=[vmem] * 2,
        compiler_params=pltpu.CompilerParams(vmem_limit_bytes=8 * MIB),
        cost_estimate=pl.CostEstimate(flops=67_000_000, bytes_accessed=MIB, transcendentals=0),
        name="query",
    )(*parts, query_weight)
    operands = [
        sink_logit,
        norm_gain.reshape(1, width),
        mixing,
        up_weight,
        down_weight,
    ]
    operands = [pltpu.with_memory_space_constraint(o, pltpu.HBM) for o in operands]
    encoded = pl.pallas_call(
        functools.partial(
            encode_kernel, block_order=[o ^ first for o in LATER for first in (0, FIRST)]
        ),
        out_shape=jax.ShapeDtypeStruct((rows, width), jnp.bfloat16),
        in_specs=[smem] + [vmem] * 6 + [far] * len(operands),
        out_specs=vmem,
        scratch_shapes=[
            (pltpu.SMEM if operand.shape[-1] == HEADS else pltpu.VMEM)(operand.shape, operand.dtype)
            for operand in operands
        ]
        + [pltpu.SemaphoreType.DMA((len(operands),))],
        compiler_params=pltpu.CompilerParams(vmem_limit_bytes=32 * MIB),
        cost_estimate=pl.CostEstimate(
            flops=1_500_000_000, bytes_accessed=5 * MIB, transcendentals=1_200_000
        ),
        name="encode",
    )(here.reshape(1), received, key_weight, value_weight, out_weight, queries, columns, *operands)
    return lax.all_to_all(
        encoded.reshape(levels, cells_here, width), "lev", split_axis=0, concat_axis=1, tiled=True
    )


def solution(mesh):
    placed = (
        P("lev", "tile", None),
        P("tile", None),
        P("tile", None),
        P("tile"),
        P(),
        P(),
        P(),
        P(),
        P(),
        P(),
        P(),
        P(),
        P(),
    )
    return jax.shard_map(
        body, mesh=mesh, in_specs=placed, out_specs=P("lev", "tile", None), check_vma=False
    )
```

```python
import functools

import jax
import jax.numpy as jnp
from jax import lax
from jax.experimental import pallas as pl
from jax.experimental.pallas import tpu as pltpu
from jax.sharding import PartitionSpec as P

SUBCELLS = 32
HEADS = 8
EMPTY = 64.0
EMPTY_FROM = 48.0
MIB = 1 << 20


FIRST = 1
LATER = (0, 2, 6, 5)


def pick(pieces, levels):
    return jnp.stack([lax.dynamic_index_in_dim(pieces, l, 0, keepdims=False) for l in levels])


def start_loads(far, near, loaded):
    loads = [pltpu.make_async_copy(f, n, loaded.at[i]) for i, (f, n) in enumerate(zip(far, near))]
    for load in loads:
        load.start()
    return loads


def fetch_kernel(
    level_here,
    pieces_hbm,
    target_hbm,
    subtile_hbm,
    tokens_hbm,
    half_ref,
    target_ref,
    subtile_ref,
    tokens_ref,
    loaded,
):
    far = [target_hbm, subtile_hbm, tokens_hbm]
    near = [target_ref, subtile_ref, tokens_ref]
    for i, offset in enumerate(LATER):
        far.append(pieces_hbm.at[level_here[0] ^ FIRST ^ offset])
        near.append(half_ref.at[i])
    for load in start_loads(far, near, loaded):
        load.wait()


def route_kernel(
    sub_here,
    target_ref,
    subtile_ref,
    tokens_ref,
    bank_ref,
    *spare_ref,
    tile_count,
    capacity,
):
    for ref in spare_ref:
        ref[...] = jnp.zeros(ref.shape, ref.dtype)
    rows = tokens_ref.shape[0]
    width = tokens_ref.shape[1]
    before = lax.broadcasted_iota(jnp.int32, (rows, rows), 0) < lax.broadcasted_iota(
        jnp.int32, (rows, rows), 1
    )
    before = jnp.where(before, 1.0, 0.0).astype(jnp.bfloat16)
    keep = jnp.abs(subtile_ref[...] - sub_here[0]) <= 1
    target = jnp.where(keep, target_ref[...], -1)
    tile_ids = lax.broadcasted_iota(jnp.int32, (tile_count, rows), 0)
    named = target == tile_ids
    onehot = jnp.where(named, 1.0, 0.0)
    rank = jnp.dot(onehot.astype(jnp.bfloat16), before, preferred_element_type=jnp.float32)
    rank = jnp.where(named, rank, -1.0)
    count = jnp.sum(onehot, axis=1, keepdims=True)
    tokens = tokens_ref[...]
    group = 8
    slot = lax.broadcasted_iota(jnp.int32, (group, capacity, rows), 1).astype(jnp.float32)
    slot_out = lax.broadcasted_iota(jnp.int32, (group, capacity, width), 1).astype(jnp.float32)
    for first in range(0, tile_count, group):
        pick = jnp.where(rank[first : first + group][:, None, :] == slot, 1.0, 0.0)
        pick = pick.reshape(group * capacity, rows).astype(jnp.bfloat16)
        taken = jnp.dot(pick, tokens, preferred_element_type=jnp.float32)
        filled = slot_out < count[first : first + group][:, None, :]
        taken = jnp.where(filled, taken.reshape(group, capacity, width), EMPTY)
        bank_ref[first * capacity : (first + group) * capacity, :] = taken.reshape(
            group * capacity, width
        ).astype(jnp.bfloat16)


def query_kernel(*refs):
    *piece_refs, weight_ref, _, _, _, columns_ref, query_ref = refs
    columns = jnp.concatenate([ref[...] for ref in piece_refs], axis=0)
    columns_ref[...] = columns
    query = jnp.dot(columns, weight_ref[...], preferred_element_type=jnp.float32)
    query_ref[...] = query.astype(jnp.bfloat16)


def encode_kernel(*refs, block_order):
    (
        level_here,
        tokens_ref,
        key_weight_ref,
        value_weight_ref,
        out_weight_ref,
        query_ref,
        grid_ref,
    ) = refs[:7]
    far, encoded_ref, near, loaded = refs[7:12], refs[12], refs[13:18], refs[18]
    sink_ref, gain_ref, mixing_ref, up_ref, down_ref = near
    loads = start_loads(far, near, loaded)
    levels = len(block_order)
    rows, width = query_ref.shape
    head_width = width // HEADS
    tokens = tokens_ref[...]
    over_tokens = (((1,), (1,)), ((), ()))
    lane = lax.broadcasted_iota(jnp.int32, (16, tokens.shape[1]), 1)
    first_feature = jnp.where(lane == 0, 1.0, 0.0).astype(jnp.bfloat16)
    marks = lax.dot_general(
        first_feature, tokens, over_tokens, preferred_element_type=jnp.float32
    )[0:1]
    bias = jnp.where(marks > EMPTY_FROM, -1e30, 0.0)
    keys = jnp.dot(tokens, key_weight_ref[...], preferred_element_type=jnp.float32).astype(
        jnp.bfloat16
    )
    values = jnp.dot(tokens, value_weight_ref[...], preferred_element_type=jnp.float32).astype(
        jnp.bfloat16
    )
    group = 2 * head_width
    lane_head = lax.broadcasted_iota(jnp.int32, (rows, group), 1) // head_width
    loads[0].wait()
    attended = []
    for p in range(HEADS // 2):
        lanes = slice(p * group, (p + 1) * group)
        query = query_ref[:, lanes].astype(jnp.float32) * head_width**-0.5
        value = values[:, lanes]
        value = jnp.concatenate([value, jnp.ones_like(value)], axis=1)
        mine = None
        for h in range(2):
            sink = sink_ref[2 * p + h]
            one = jnp.where(lane_head == h, query, 0.0).astype(jnp.bfloat16)
            scores = bias + lax.dot_general(
                one, keys[:, lanes], over_tokens, preferred_element_type=jnp.float32
            )
            peak = jnp.maximum(jnp.max(scores, axis=1, keepdims=True), sink)
            weights = jnp.exp(scores - peak)
            mixed = jnp.dot(weights.astype(jnp.bfloat16), value, preferred_element_type=jnp.float32)
            mixed = mixed[:, :group] / (mixed[:, group:] + jnp.exp(sink - peak))
            mine = mixed if mine is None else jnp.where(lane_head == h, mixed, mine)
        attended.append(mine.astype(jnp.bfloat16))
    attended = jnp.concatenate(attended, axis=1)
    updated = (
        grid_ref[...].astype(jnp.float32)
        + jnp.dot(attended, out_weight_ref[...], preferred_element_type=jnp.float32)
    ).astype(jnp.bfloat16)
    wide = updated.astype(jnp.float32)
    loads[1].wait()
    loads[2].wait()
    inverse = lax.rsqrt(jnp.mean(wide * wide, axis=1, keepdims=True) + 1e-05)
    normed = wide * inverse * gain_ref[...]
    cells = rows // levels
    parts = [normed[m * cells : (m + 1) * cells] for m in range(levels)]
    held = [level_here[0] ^ offset for offset in block_order]
    blended = []
    for l in held:
        total = mixing_ref[l, held[0]] * parts[0]
        for m in range(1, levels):
            total = total + mixing_ref[l, held[m]] * parts[m]
        blended.append(total)
    blended = jnp.concatenate(blended, axis=0).astype(jnp.bfloat16)
    loads[3].wait()
    hidden = jax.nn.gelu(
        jnp.dot(blended, up_ref[...], preferred_element_type=jnp.float32)
    ).astype(jnp.bfloat16)
    loads[4].wait()
    encoded = (
        wide + jnp.dot(hidden, down_ref[...], preferred_element_type=jnp.float32)
    ).astype(jnp.bfloat16)
    for e, l in enumerate(held):
        start = pl.multiple_of(l * cells, cells)
        encoded_ref[pl.ds(start, cells), :] = encoded[e * cells : (e + 1) * cells]


def exchange_permute(array, offset, count):
    return lax.ppermute(array, "lev", [(i, i ^ offset) for i in range(count)])


def body(
    grid_state,
    observations,
    destination,
    subtile,
    query_weight,
    key_weight,
    value_weight,
    out_weight,
    sink_logit,
    norm_gain,
    mixing,
    up_weight,
    down_weight,
):
    tile_count = lax.axis_size("tile")
    levels = lax.axis_size("lev")
    token_rows, token_width = observations.shape
    capacity = 2 * token_rows // tile_count
    cells, width = grid_state.shape[1:]
    cells_here = cells // levels
    rows = levels * cells_here
    sub_here = (lax.axis_index("lev") * cells_here // SUBCELLS).reshape(1)
    smem = pl.BlockSpec(memory_space=pltpu.SMEM)
    vmem = pl.BlockSpec(memory_space=pltpu.VMEM)
    far = pl.BlockSpec(memory_space=pl.ANY)

    here = lax.axis_index("lev")
    pieces = grid_state.reshape(levels, cells_here, width)
    half, target, subtile_row, tokens = pl.pallas_call(
        fetch_kernel,
        out_shape=[
            pltpu.VMEM((len(LATER), cells_here, width), grid_state.dtype),
            pltpu.VMEM((1, token_rows), jnp.int32),
            pltpu.VMEM((1, token_rows), jnp.int32),
            pltpu.VMEM(observations.shape, observations.dtype),
        ],
        in_specs=[smem] + [far] * 4,
        out_specs=[vmem] * 4,
        scratch_shapes=[pltpu.SemaphoreType.DMA((3 + len(LATER),))],
        compiler_params=pltpu.CompilerParams(vmem_limit_bytes=8 * MIB),
        cost_estimate=pl.CostEstimate(flops=1000, bytes_accessed=MIB, transcendentals=0),
        name="fetch",
    )(
        here.reshape(1),
        *(
            pltpu.with_memory_space_constraint(o, pltpu.HBM)
            for o in (
                pieces,
                destination.reshape(1, token_rows),
                subtile.reshape(1, token_rows),
                observations,
            )
        ),
    )
    bank_shape = jax.ShapeDtypeStruct((tile_count * capacity, token_width), observations.dtype)
    half_shape = jax.ShapeDtypeStruct(half.shape, half.dtype)

    def route(out_shape):
        return pl.pallas_call(
            functools.partial(route_kernel, tile_count=tile_count, capacity=capacity),
            out_shape=out_shape,
            in_specs=[smem] + [vmem] * 3,
            out_specs=[vmem] * len(out_shape),
            compiler_params=pltpu.CompilerParams(vmem_limit_bytes=32 * MIB),
            cost_estimate=pl.CostEstimate(
                flops=300_000_000, bytes_accessed=MIB, transcendentals=0
            ),
            name="route",
        )

    early = (lax.axis_index("tile") // 2) % 8 < 3
    bank, came = lax.cond(
        early,
        lambda h, *of: (route([bank_shape])(*of)[0], exchange_permute(h, FIRST, levels)),
        lambda h, *of: tuple(route([bank_shape, half_shape])(*of)),
        half,
        sub_here,
        target,
        subtile_row,
        tokens,
    )
    bank, came = lax.optimization_barrier((bank, came))
    received = lax.all_to_all(
        bank.reshape(tile_count, capacity, token_width),
        "tile",
        split_axis=0,
        concat_axis=0,
        tiled=True,
    ).reshape(tile_count * capacity, token_width)
    came_late = lax.cond(
        early, jnp.zeros_like, lambda h: exchange_permute(h, FIRST, levels), half
    )
    came = jnp.where(early, came, came_late)
    parts = []
    for came_block, offset in zip(came, LATER):
        both = jnp.stack([pick(pieces, [here ^ offset])[0], came_block])
        both = both.reshape(2 * cells_here, width)
        parts.append(both if offset == 0 else exchange_permute(both, offset, levels))
    columns, queries = pl.pallas_call(
        query_kernel,
        out_shape=[jax.ShapeDtypeStruct((rows, width), jnp.bfloat16)] * 2,
        in_specs=[vmem] * (len(parts) + 4),
        out_specs=[vmem] * 2,
        compiler_params=pltpu.CompilerParams(vmem_limit_bytes=8 * MIB),
        cost_estimate=pl.CostEstimate(flops=67_000_000, bytes_accessed=MIB, transcendentals=0),
        name="query",
    )(*parts, query_weight, key_weight, value_weight, out_weight)
    operands = [
        sink_logit,
        norm_gain.reshape(1, width),
        mixing,
        up_weight,
        down_weight,
    ]
    operands = [pltpu.with_memory_space_constraint(o, pltpu.HBM) for o in operands]
    encoded = pl.pallas_call(
        functools.partial(
            encode_kernel, block_order=[o ^ first for o in LATER for first in (0, FIRST)]
        ),
        out_shape=jax.ShapeDtypeStruct((rows, width), jnp.bfloat16),
        in_specs=[smem] + [vmem] * 6 + [far] * len(operands),
        out_specs=vmem,
        scratch_shapes=[
            (pltpu.SMEM if operand.shape[-1] == HEADS else pltpu.VMEM)(operand.shape, operand.dtype)
            for operand in operands
        ]
        + [pltpu.SemaphoreType.DMA((len(operands),))],
        compiler_params=pltpu.CompilerParams(vmem_limit_bytes=32 * MIB),
        cost_estimate=pl.CostEstimate(
            flops=1_500_000_000, bytes_accessed=5 * MIB, transcendentals=1_200_000
        ),
        name="encode",
    )(here.reshape(1), received, key_weight, value_weight, out_weight, queries, columns, *operands)
    return lax.all_to_all(
        encoded.reshape(levels, cells_here, width), "lev", split_axis=0, concat_axis=1, tiled=True
    )


def solution(mesh):
    placed = (
        P("lev", "tile", None),
        P("tile", None),
        P("tile", None),
        P("tile"),
        P(),
        P(),
        P(),
        P(),
        P(),
        P(),
        P(),
        P(),
        P(),
    )
    return jax.shard_map(
        body, mesh=mesh, in_specs=placed, out_specs=P("lev", "tile", None), check_vma=False
    )
```

```python
import functools

import jax
import jax.numpy as jnp
from jax import lax
from jax.experimental import pallas as pl
from jax.experimental.pallas import tpu as pltpu
from jax.sharding import PartitionSpec as P

SUBCELLS = 32
HEADS = 8
EMPTY = 64.0
EMPTY_FROM = 48.0
MIB = 1 << 20


FIRST = 1
LATER = (0, 2, 5, 6)


def pick(pieces, levels):
    return jnp.stack([lax.dynamic_index_in_dim(pieces, l, 0, keepdims=False) for l in levels])


def start_loads(far, near, loaded):
    loads = [pltpu.make_async_copy(f, n, loaded.at[i]) for i, (f, n) in enumerate(zip(far, near))]
    for load in loads:
        load.start()
    return loads


def fetch_kernel(
    level_here,
    pieces_hbm,
    target_hbm,
    subtile_hbm,
    tokens_hbm,
    half_ref,
    target_ref,
    subtile_ref,
    tokens_ref,
    loaded,
):
    far = [target_hbm, subtile_hbm, tokens_hbm]
    near = [target_ref, subtile_ref, tokens_ref]
    for i, offset in enumerate(LATER):
        far.append(pieces_hbm.at[level_here[0] ^ FIRST ^ offset])
        near.append(half_ref.at[i])
    for load in start_loads(far, near, loaded):
        load.wait()


def route_kernel(
    sub_here,
    target_ref,
    subtile_ref,
    tokens_ref,
    bank_ref,
    *spare_ref,
    tile_count,
    capacity,
):
    for ref in spare_ref:
        ref[...] = jnp.zeros(ref.shape, ref.dtype)
    rows = tokens_ref.shape[0]
    width = tokens_ref.shape[1]
    before = lax.broadcasted_iota(jnp.int32, (rows, rows), 0) < lax.broadcasted_iota(
        jnp.int32, (rows, rows), 1
    )
    before = jnp.where(before, 1.0, 0.0).astype(jnp.bfloat16)
    keep = jnp.abs(subtile_ref[...] - sub_here[0]) <= 1
    target = jnp.where(keep, target_ref[...], -1)
    tile_ids = lax.broadcasted_iota(jnp.int32, (tile_count, rows), 0)
    named = target == tile_ids
    onehot = jnp.where(named, 1.0, 0.0)
    rank = jnp.dot(onehot.astype(jnp.bfloat16), before, preferred_element_type=jnp.float32)
    rank = jnp.where(named, rank, -1.0)
    count = jnp.sum(onehot, axis=1, keepdims=True)
    tokens = tokens_ref[...]
    group = 8
    slot = lax.broadcasted_iota(jnp.int32, (group, capacity, rows), 1).astype(jnp.float32)
    slot_out = lax.broadcasted_iota(jnp.int32, (group, capacity, width), 1).astype(jnp.float32)
    for first in range(0, tile_count, group):
        pick = jnp.where(rank[first : first + group][:, None, :] == slot, 1.0, 0.0)
        pick = pick.reshape(group * capacity, rows).astype(jnp.bfloat16)
        taken = jnp.dot(pick, tokens, preferred_element_type=jnp.float32)
        filled = slot_out < count[first : first + group][:, None, :]
        taken = jnp.where(filled, taken.reshape(group, capacity, width), EMPTY)
        bank_ref[first * capacity : (first + group) * capacity, :] = taken.reshape(
            group * capacity, width
        ).astype(jnp.bfloat16)


def query_kernel(*refs):
    *piece_refs, weight_ref, _, _, _, columns_ref, query_ref = refs
    columns = jnp.concatenate([ref[...] for ref in piece_refs], axis=0)
    columns_ref[...] = columns
    query = jnp.dot(columns, weight_ref[...], preferred_element_type=jnp.float32)
    query_ref[...] = query.astype(jnp.bfloat16)


def encode_kernel(*refs, block_order):
    (
        level_here,
        tokens_ref,
        key_weight_ref,
        value_weight_ref,
        out_weight_ref,
        query_ref,
        grid_ref,
    ) = refs[:7]
    far, encoded_ref, near, loaded = refs[7:12], refs[12], refs[13:18], refs[18]
    sink_ref, gain_ref, mixing_ref, up_ref, down_ref = near
    loads = start_loads(far, near, loaded)
    levels = len(block_order)
    rows, width = query_ref.shape
    head_width = width // HEADS
    tokens = tokens_ref[...]
    over_tokens = (((1,), (1,)), ((), ()))
    lane = lax.broadcasted_iota(jnp.int32, (16, tokens.shape[1]), 1)
    first_feature = jnp.where(lane == 0, 1.0, 0.0).astype(jnp.bfloat16)
    marks = lax.dot_general(
        first_feature, tokens, over_tokens, preferred_element_type=jnp.float32
    )[0:1]
    bias = jnp.where(marks > EMPTY_FROM, -1e30, 0.0)
    keys = jnp.dot(tokens, key_weight_ref[...], preferred_element_type=jnp.float32).astype(
        jnp.bfloat16
    )
    values = jnp.dot(tokens, value_weight_ref[...], preferred_element_type=jnp.float32).astype(
        jnp.bfloat16
    )
    group = 2 * head_width
    lane_head = lax.broadcasted_iota(jnp.int32, (rows, group), 1) // head_width
    loads[0].wait()
    attended = []
    for p in range(HEADS // 2):
        lanes = slice(p * group, (p + 1) * group)
        query = query_ref[:, lanes].astype(jnp.float32) * head_width**-0.5
        value = values[:, lanes]
        value = jnp.concatenate([value, jnp.ones_like(value)], axis=1)
        mine = None
        for h in range(2):
            sink = sink_ref[2 * p + h]
            one = jnp.where(lane_head == h, query, 0.0).astype(jnp.bfloat16)
            scores = bias + lax.dot_general(
                one, keys[:, lanes], over_tokens, preferred_element_type=jnp.float32
            )
            peak = jnp.maximum(jnp.max(scores, axis=1, keepdims=True), sink)
            weights = jnp.exp(scores - peak)
            mixed = jnp.dot(weights.astype(jnp.bfloat16), value, preferred_element_type=jnp.float32)
            mixed = mixed[:, :group] / (mixed[:, group:] + jnp.exp(sink - peak))
            mine = mixed if mine is None else jnp.where(lane_head == h, mixed, mine)
        attended.append(mine.astype(jnp.bfloat16))
    attended = jnp.concatenate(attended, axis=1)
    updated = (
        grid_ref[...].astype(jnp.float32)
        + jnp.dot(attended, out_weight_ref[...], preferred_element_type=jnp.float32)
    ).astype(jnp.bfloat16)
    wide = updated.astype(jnp.float32)
    loads[1].wait()
    loads[2].wait()
    inverse = lax.rsqrt(jnp.mean(wide * wide, axis=1, keepdims=True) + 1e-05)
    normed = wide * inverse * gain_ref[...]
    cells = rows // levels
    parts = [normed[m * cells : (m + 1) * cells] for m in range(levels)]
    held = [level_here[0] ^ offset for offset in block_order]
    blended = []
    for l in held:
        total = mixing_ref[l, held[0]] * parts[0]
        for m in range(1, levels):
            total = total + mixing_ref[l, held[m]] * parts[m]
        blended.append(total)
    blended = jnp.concatenate(blended, axis=0).astype(jnp.bfloat16)
    loads[3].wait()
    hidden = jax.nn.gelu(
        jnp.dot(blended, up_ref[...], preferred_element_type=jnp.float32)
    ).astype(jnp.bfloat16)
    loads[4].wait()
    encoded = (
        wide + jnp.dot(hidden, down_ref[...], preferred_element_type=jnp.float32)
    ).astype(jnp.bfloat16)
    for e, l in enumerate(held):
        start = pl.multiple_of(l * cells, cells)
        encoded_ref[pl.ds(start, cells), :] = encoded[e * cells : (e + 1) * cells]


def exchange_permute(array, offset, count):
    return lax.ppermute(array, "lev", [(i, i ^ offset) for i in range(count)])


def body(
    grid_state,
    observations,
    destination,
    subtile,
    query_weight,
    key_weight,
    value_weight,
    out_weight,
    sink_logit,
    norm_gain,
    mixing,
    up_weight,
    down_weight,
):
    tile_count = lax.axis_size("tile")
    levels = lax.axis_size("lev")
    token_rows, token_width = observations.shape
    capacity = 2 * token_rows // tile_count
    cells, width = grid_state.shape[1:]
    cells_here = cells // levels
    rows = levels * cells_here
    sub_here = (lax.axis_index("lev") * cells_here // SUBCELLS).reshape(1)
    smem = pl.BlockSpec(memory_space=pltpu.SMEM)
    vmem = pl.BlockSpec(memory_space=pltpu.VMEM)
    far = pl.BlockSpec(memory_space=pl.ANY)

    here = lax.axis_index("lev")
    pieces = grid_state.reshape(levels, cells_here, width)
    half, target, subtile_row, tokens = pl.pallas_call(
        fetch_kernel,
        out_shape=[
            pltpu.VMEM((len(LATER), cells_here, width), grid_state.dtype),
            pltpu.VMEM((1, token_rows), jnp.int32),
            pltpu.VMEM((1, token_rows), jnp.int32),
            pltpu.VMEM(observations.shape, observations.dtype),
        ],
        in_specs=[smem] + [far] * 4,
        out_specs=[vmem] * 4,
        scratch_shapes=[pltpu.SemaphoreType.DMA((3 + len(LATER),))],
        compiler_params=pltpu.CompilerParams(vmem_limit_bytes=8 * MIB),
        cost_estimate=pl.CostEstimate(flops=1000, bytes_accessed=MIB, transcendentals=0),
        name="fetch",
    )(
        here.reshape(1),
        *(
            pltpu.with_memory_space_constraint(o, pltpu.HBM)
            for o in (
                pieces,
                destination.reshape(1, token_rows),
                subtile.reshape(1, token_rows),
                observations,
            )
        ),
    )
    bank_shape = jax.ShapeDtypeStruct((tile_count * capacity, token_width), observations.dtype)
    half_shape = jax.ShapeDtypeStruct(half.shape, half.dtype)

    def route(out_shape):
        return pl.pallas_call(
            functools.partial(route_kernel, tile_count=tile_count, capacity=capacity),
            out_shape=out_shape,
            in_specs=[smem] + [vmem] * 3,
            out_specs=[vmem] * len(out_shape),
            compiler_params=pltpu.CompilerParams(vmem_limit_bytes=32 * MIB),
            cost_estimate=pl.CostEstimate(
                flops=300_000_000, bytes_accessed=MIB, transcendentals=0
            ),
            name="route",
        )

    early = (lax.axis_index("tile") // 2) % 8 < 3
    bank, came = lax.cond(
        early,
        lambda h, *of: (route([bank_shape])(*of)[0], exchange_permute(h, FIRST, levels)),
        lambda h, *of: tuple(route([bank_shape, half_shape])(*of)),
        half,
        sub_here,
        target,
        subtile_row,
        tokens,
    )
    bank, came = lax.optimization_barrier((bank, came))
    received = lax.all_to_all(
        bank.reshape(tile_count, capacity, token_width),
        "tile",
        split_axis=0,
        concat_axis=0,
        tiled=True,
    ).reshape(tile_count * capacity, token_width)
    came_late = lax.cond(
        early, jnp.zeros_like, lambda h: exchange_permute(h, FIRST, levels), half
    )
    came = jnp.where(early, came, came_late)
    parts = []
    for came_block, offset in zip(came, LATER):
        both = jnp.stack([pick(pieces, [here ^ offset])[0], came_block])
        both = both.reshape(2 * cells_here, width)
        parts.append(both if offset == 0 else exchange_permute(both, offset, levels))
    columns, queries = pl.pallas_call(
        query_kernel,
        out_shape=[jax.ShapeDtypeStruct((rows, width), jnp.bfloat16)] * 2,
        in_specs=[vmem] * (len(parts) + 4),
        out_specs=[vmem] * 2,
        compiler_params=pltpu.CompilerParams(vmem_limit_bytes=8 * MIB),
        cost_estimate=pl.CostEstimate(flops=67_000_000, bytes_accessed=MIB, transcendentals=0),
        name="query",
    )(*parts, query_weight, key_weight, value_weight, out_weight)
    operands = [
        sink_logit,
        norm_gain.reshape(1, width),
        mixing,
        up_weight,
        down_weight,
    ]
    operands = [pltpu.with_memory_space_constraint(o, pltpu.HBM) for o in operands]
    encoded = pl.pallas_call(
        functools.partial(
            encode_kernel, block_order=[o ^ first for o in LATER for first in (0, FIRST)]
        ),
        out_shape=jax.ShapeDtypeStruct((rows, width), jnp.bfloat16),
        in_specs=[smem] + [vmem] * 6 + [far] * len(operands),
        out_specs=vmem,
        scratch_shapes=[
            (pltpu.SMEM if operand.shape[-1] == HEADS else pltpu.VMEM)(operand.shape, operand.dtype)
            for operand in operands
        ]
        + [pltpu.SemaphoreType.DMA((len(operands),))],
        compiler_params=pltpu.CompilerParams(vmem_limit_bytes=32 * MIB),
        cost_estimate=pl.CostEstimate(
            flops=1_500_000_000, bytes_accessed=5 * MIB, transcendentals=1_200_000
        ),
        name="encode",
    )(here.reshape(1), received, key_weight, value_weight, out_weight, queries, columns, *operands)
    return lax.all_to_all(
        encoded.reshape(levels, cells_here, width), "lev", split_axis=0, concat_axis=1, tiled=True
    )


def solution(mesh):
    placed = (
        P("lev", "tile", None),
        P("tile", None),
        P("tile", None),
        P("tile"),
        P(),
        P(),
        P(),
        P(),
        P(),
        P(),
        P(),
        P(),
        P(),
    )
    return jax.shard_map(
        body, mesh=mesh, in_specs=placed, out_specs=P("lev", "tile", None), check_vma=False
    )
```

```python
import functools

import jax
import jax.numpy as jnp
from jax import lax
from jax.experimental import pallas as pl
from jax.experimental.pallas import tpu as pltpu
from jax.sharding import PartitionSpec as P

SUBCELLS = 32
HEADS = 8
EMPTY = 64.0
EMPTY_FROM = 48.0
MIB = 1 << 20
GROUP = 8


FIRST = 1
LATER = (0, 6, 5, 2)


def pick(pieces, levels):
    return jnp.stack([lax.dynamic_index_in_dim(pieces, l, 0, keepdims=False) for l in levels])


def start_loads(far, near, loaded):
    loads = [pltpu.make_async_copy(f, n, loaded.at[i]) for i, (f, n) in enumerate(zip(far, near))]
    for load in loads:
        load.start()
    return loads


def half_kernel(level_here, pieces_hbm, half_ref, loaded):
    far = [pieces_hbm.at[level_here[0] ^ FIRST ^ offset] for offset in LATER]
    for load in start_loads(far, [half_ref.at[i] for i in range(len(LATER))], loaded):
        load.wait()


def fetch_kernel(
    level_here,
    target_hbm,
    subtile_hbm,
    tokens_hbm,
    pieces_hbm,
    target_ref,
    subtile_ref,
    tokens_ref,
    half_ref,
    loaded,
):
    far = [target_hbm, subtile_hbm, tokens_hbm]
    near = [target_ref, subtile_ref, tokens_ref]
    for i, offset in enumerate(LATER):
        far.append(pieces_hbm.at[level_here[0] ^ FIRST ^ offset])
        near.append(half_ref.at[i])
    for load in start_loads(far, near, loaded):
        load.wait()


def fill_bank(sub_here, target_ref, subtile_ref, tokens_ref, bank_ref, loads, tile_count, capacity):
    rows = tokens_ref.shape[0]
    width = tokens_ref.shape[1]
    before = lax.broadcasted_iota(jnp.int32, (rows, rows), 0) < lax.broadcasted_iota(
        jnp.int32, (rows, rows), 1
    )
    before = jnp.where(before, 1.0, 0.0).astype(jnp.bfloat16)
    for load in loads[:2]:
        load.wait()
    keep = jnp.abs(subtile_ref[...] - sub_here[0]) <= 1
    target = jnp.where(keep, target_ref[...], -1)
    tile_ids = lax.broadcasted_iota(jnp.int32, (tile_count, rows), 0)
    named = target == tile_ids
    onehot = jnp.where(named, 1.0, 0.0)
    rank = jnp.dot(onehot.astype(jnp.bfloat16), before, preferred_element_type=jnp.float32)
    rank = jnp.where(named, rank, -1.0)
    count = jnp.sum(onehot, axis=1, keepdims=True)
    for load in loads[2:]:
        load.wait()
    tokens = tokens_ref[...]
    group = GROUP
    slot = lax.broadcasted_iota(jnp.int32, (group, capacity, rows), 1).astype(jnp.float32)
    slot_out = lax.broadcasted_iota(jnp.int32, (group, capacity, width), 1).astype(jnp.float32)
    for first in range(0, tile_count, group):
        pick = jnp.where(rank[first : first + group][:, None, :] == slot, 1.0, 0.0)
        pick = pick.reshape(group * capacity, rows).astype(jnp.bfloat16)
        taken = jnp.dot(pick, tokens, preferred_element_type=jnp.float32)
        filled = slot_out < count[first : first + group][:, None, :]
        taken = jnp.where(filled, taken.reshape(group, capacity, width), EMPTY)
        bank_ref[first * capacity : (first + group) * capacity, :] = taken.reshape(
            group * capacity, width
        ).astype(jnp.bfloat16)


def route_early_kernel(
    sub_here,
    target_hbm,
    subtile_hbm,
    tokens_hbm,
    bank_ref,
    target_ref,
    subtile_ref,
    tokens_ref,
    loaded,
    **sizes,
):
    near = (target_ref, subtile_ref, tokens_ref)
    loads = start_loads((target_hbm, subtile_hbm, tokens_hbm), near, loaded)
    fill_bank(sub_here, *near, bank_ref, loads, **sizes)


def route_late_kernel(
    sub_here, target_ref, subtile_ref, tokens_ref, half_ref, bank_ref, half_out_ref, **sizes
):
    half_out_ref[...] = half_ref[...]
    fill_bank(sub_here, target_ref, subtile_ref, tokens_ref, bank_ref, [], **sizes)


def query_kernel(*refs):
    *piece_refs, weight_ref, _, _, _, columns_ref, query_ref = refs
    columns = jnp.concatenate([ref[...] for ref in piece_refs], axis=0)
    columns_ref[...] = columns
    query = jnp.dot(columns, weight_ref[...], preferred_element_type=jnp.float32)
    query_ref[...] = query.astype(jnp.bfloat16)


def encode_kernel(*refs, block_order):
    (
        level_here,
        tokens_ref,
        key_weight_ref,
        value_weight_ref,
        out_weight_ref,
        query_ref,
        grid_ref,
    ) = refs[:7]
    far, encoded_ref, near, loaded = refs[7:12], refs[12], refs[13:18], refs[18]
    sink_ref, gain_ref, mixing_ref, up_ref, down_ref = near
    loads = start_loads(far, near, loaded)
    levels = len(block_order)
    rows, width = query_ref.shape
    head_width = width // HEADS
    tokens = tokens_ref[...]
    over_tokens = (((1,), (1,)), ((), ()))
    lane = lax.broadcasted_iota(jnp.int32, (16, tokens.shape[1]), 1)
    first_feature = jnp.where(lane == 0, 1.0, 0.0).astype(jnp.bfloat16)
    marks = lax.dot_general(
        first_feature, tokens, over_tokens, preferred_element_type=jnp.float32
    )[0:1]
    bias = jnp.where(marks > EMPTY_FROM, -1e30, 0.0)
    keys = jnp.dot(tokens, key_weight_ref[...], preferred_element_type=jnp.float32).astype(
        jnp.bfloat16
    )
    values = jnp.dot(tokens, value_weight_ref[...], preferred_element_type=jnp.float32).astype(
        jnp.bfloat16
    )
    group = 2 * head_width
    lane_head = lax.broadcasted_iota(jnp.int32, (rows, group), 1) // head_width
    loads[0].wait()
    attended = []
    for p in range(HEADS // 2):
        lanes = slice(p * group, (p + 1) * group)
        query = query_ref[:, lanes].astype(jnp.float32) * head_width**-0.5
        value = values[:, lanes]
        value = jnp.concatenate([value, jnp.ones_like(value)], axis=1)
        mine = None
        for h in range(2):
            sink = sink_ref[2 * p + h]
            one = jnp.where(lane_head == h, query, 0.0).astype(jnp.bfloat16)
            scores = bias + lax.dot_general(
                one, keys[:, lanes], over_tokens, preferred_element_type=jnp.float32
            )
            peak = jnp.maximum(jnp.max(scores, axis=1, keepdims=True), sink)
            weights = jnp.exp(scores - peak)
            mixed = jnp.dot(weights.astype(jnp.bfloat16), value, preferred_element_type=jnp.float32)
            mixed = mixed[:, :group] / (mixed[:, group:] + jnp.exp(sink - peak))
            mine = mixed if mine is None else jnp.where(lane_head == h, mixed, mine)
        attended.append(mine.astype(jnp.bfloat16))
    attended = jnp.concatenate(attended, axis=1)
    updated = (
        grid_ref[...].astype(jnp.float32)
        + jnp.dot(attended, out_weight_ref[...], preferred_element_type=jnp.float32)
    ).astype(jnp.bfloat16)
    wide = updated.astype(jnp.float32)
    loads[1].wait()
    loads[2].wait()
    inverse = lax.rsqrt(jnp.mean(wide * wide, axis=1, keepdims=True) + 1e-05)
    normed = wide * inverse * gain_ref[...]
    cells = rows // levels
    parts = [normed[m * cells : (m + 1) * cells] for m in range(levels)]
    held = [level_here[0] ^ offset for offset in block_order]
    blended = []
    for l in held:
        total = mixing_ref[l, held[0]] * parts[0]
        for m in range(1, levels):
            total = total + mixing_ref[l, held[m]] * parts[m]
        blended.append(total)
    blended = jnp.concatenate(blended, axis=0).astype(jnp.bfloat16)
    loads[3].wait()
    hidden = jax.nn.gelu(
        jnp.dot(blended, up_ref[...], preferred_element_type=jnp.float32)
    ).astype(jnp.bfloat16)
    loads[4].wait()
    encoded = (
        wide + jnp.dot(hidden, down_ref[...], preferred_element_type=jnp.float32)
    ).astype(jnp.bfloat16)
    for e, l in enumerate(held):
        start = pl.multiple_of(l * cells, cells)
        encoded_ref[pl.ds(start, cells), :] = encoded[e * cells : (e + 1) * cells]


def exchange_permute(array, offset, count):
    return lax.ppermute(array, "lev", [(i, i ^ offset) for i in range(count)])


def body(
    grid_state,
    observations,
    destination,
    subtile,
    query_weight,
    key_weight,
    value_weight,
    out_weight,
    sink_logit,
    norm_gain,
    mixing,
    up_weight,
    down_weight,
):
    tile_count = lax.axis_size("tile")
    levels = lax.axis_size("lev")
    token_rows, token_width = observations.shape
    capacity = 2 * token_rows // tile_count
    cells, width = grid_state.shape[1:]
    cells_here = cells // levels
    rows = levels * cells_here
    sub_here = (lax.axis_index("lev") * cells_here // SUBCELLS).reshape(1)
    smem = pl.BlockSpec(memory_space=pltpu.SMEM)
    vmem = pl.BlockSpec(memory_space=pltpu.VMEM)
    far = pl.BlockSpec(memory_space=pl.ANY)

    here = lax.axis_index("lev")
    pieces = grid_state.reshape(levels, cells_here, width)
    bank_shape = jax.ShapeDtypeStruct((tile_count * capacity, token_width), observations.dtype)
    half_shape = jax.ShapeDtypeStruct((len(LATER), cells_here, width), grid_state.dtype)

    sizes = dict(tile_count=tile_count, capacity=capacity)
    near_shapes = [
        pltpu.VMEM((1, token_rows), jnp.int32),
        pltpu.VMEM((1, token_rows), jnp.int32),
        pltpu.VMEM(observations.shape, observations.dtype),
    ]
    small = dict(
        compiler_params=pltpu.CompilerParams(vmem_limit_bytes=8 * MIB),
        cost_estimate=pl.CostEstimate(flops=1000, bytes_accessed=MIB, transcendentals=0),
    )
    large = dict(
        compiler_params=pltpu.CompilerParams(vmem_limit_bytes=32 * MIB),
        cost_estimate=pl.CostEstimate(flops=300_000_000, bytes_accessed=MIB, transcendentals=0),
    )

    def in_hbm(arrays):
        return [pltpu.with_memory_space_constraint(a, pltpu.HBM) for a in arrays]

    def route_early(level, sub, *arrays):
        half = pl.pallas_call(
            half_kernel,
            out_shape=half_shape,
            in_specs=[smem, far],
            out_specs=vmem,
            scratch_shapes=[pltpu.SemaphoreType.DMA((len(LATER),))],
            name="half",
            **small,
        )(level, *in_hbm(arrays[3:]))
        came = exchange_permute(half, FIRST, levels)
        bank = pl.pallas_call(
            functools.partial(route_early_kernel, **sizes),
            out_shape=bank_shape,
            in_specs=[smem] + [far] * 3,
            out_specs=vmem,
            scratch_shapes=near_shapes + [pltpu.SemaphoreType.DMA((3,))],
            name="route_early",
            **large,
        )(sub, *in_hbm(arrays[:3]))
        return bank, came

    def route_late(level, sub, *arrays):
        near = pl.pallas_call(
            fetch_kernel,
            out_shape=near_shapes + [pltpu.VMEM(half_shape.shape, half_shape.dtype)],
            in_specs=[smem] + [far] * 4,
            out_specs=[vmem] * 4,
            scratch_shapes=[pltpu.SemaphoreType.DMA((3 + len(LATER),))],
            name="fetch",
            **small,
        )(level, *in_hbm(arrays))
        bank, half = pl.pallas_call(
            functools.partial(route_late_kernel, **sizes),
            out_shape=[bank_shape, half_shape],
            in_specs=[smem] + [vmem] * 4,
            out_specs=[vmem] * 2,
            name="route_late",
            **large,
        )(sub, *near)
        return bank, half

    early = (lax.axis_index("tile") // 2) % 8 < 3
    bank, came = lax.cond(
        early,
        route_early,
        route_late,
        here.reshape(1),
        sub_here,
        destination.reshape(1, token_rows),
        subtile.reshape(1, token_rows),
        observations,
        pieces,
    )
    bank, came = lax.optimization_barrier((bank, came))
    received = lax.all_to_all(
        bank.reshape(tile_count, capacity, token_width),
        "tile",
        split_axis=0,
        concat_axis=0,
        tiled=True,
    ).reshape(tile_count * capacity, token_width)
    came_late = lax.cond(
        early, jnp.zeros_like, lambda h: exchange_permute(h, FIRST, levels), came
    )
    came = jnp.where(early, came, came_late)
    parts = []
    for came_block, offset in zip(came, LATER):
        both = jnp.stack([pick(pieces, [here ^ offset])[0], came_block])
        both = both.reshape(2 * cells_here, width)
        parts.append(both if offset == 0 else exchange_permute(both, offset, levels))
    columns, queries = pl.pallas_call(
        query_kernel,
        out_shape=[jax.ShapeDtypeStruct((rows, width), jnp.bfloat16)] * 2,
        in_specs=[vmem] * (len(parts) + 4),
        out_specs=[vmem] * 2,
        compiler_params=pltpu.CompilerParams(vmem_limit_bytes=8 * MIB),
        cost_estimate=pl.CostEstimate(flops=67_000_000, bytes_accessed=MIB, transcendentals=0),
        name="query",
    )(*parts, query_weight, key_weight, value_weight, out_weight)
    operands = [
        sink_logit,
        norm_gain.reshape(1, width),
        mixing,
        up_weight,
        down_weight,
    ]
    operands = [pltpu.with_memory_space_constraint(o, pltpu.HBM) for o in operands]
    encoded = pl.pallas_call(
        functools.partial(
            encode_kernel, block_order=[o ^ first for o in LATER for first in (0, FIRST)]
        ),
        out_shape=jax.ShapeDtypeStruct((rows, width), jnp.bfloat16),
        in_specs=[smem] + [vmem] * 6 + [far] * len(operands),
        out_specs=vmem,
        scratch_shapes=[
            (pltpu.SMEM if operand.shape[-1] == HEADS else pltpu.VMEM)(operand.shape, operand.dtype)
            for operand in operands
        ]
        + [pltpu.SemaphoreType.DMA((len(operands),))],
        compiler_params=pltpu.CompilerParams(vmem_limit_bytes=32 * MIB),
        cost_estimate=pl.CostEstimate(
            flops=1_500_000_000, bytes_accessed=5 * MIB, transcendentals=1_200_000
        ),
        name="encode",
    )(here.reshape(1), received, key_weight, value_weight, out_weight, queries, columns, *operands)
    return lax.all_to_all(
        encoded.reshape(levels, cells_here, width), "lev", split_axis=0, concat_axis=1, tiled=True
    )


def solution(mesh):
    placed = (
        P("lev", "tile", None),
        P("tile", None),
        P("tile", None),
        P("tile"),
        P(),
        P(),
        P(),
        P(),
        P(),
        P(),
        P(),
        P(),
        P(),
    )
    return jax.shard_map(
        body, mesh=mesh, in_specs=placed, out_specs=P("lev", "tile", None), check_vma=False
    )
```
